128 devices in a mesh: rep: 8 (over x_hi, z), tp: 16 (over x_lo, y, core).
Axes of the slice: x: 4 (x_hi: 2, x_lo: 2; x = x_hi * 2 + x_lo), y: 4, z: 4, core: 2. Of those that a mesh axis runs over, the one named last changes fastest.
Arguments:
- inputs: bfloat16 [12288, 2560], P(('rep', 'tp')), may hold values from -6 to 6
- gate_pre: bfloat16 [12288, 14336], P('rep', 'tp'), may hold values from -6 to 6
- grad_hidden: bfloat16 [12288, 14336], P('rep', 'tp'), may hold values from -6 to 6
- up_weight: bfloat16 [8, 2560, 14336], P('rep', None, 'tp'), may hold values from -6 to 6
- momentum: bfloat16 [8, 2560, 14336], P('rep', None, 'tp'), may hold values from -4 to 4
Outputs:
- input_grad: bfloat16 [12288, 2560], P(('rep', 'tp'))
- mixed_weight: bfloat16 [8, 2560, 14336], P('rep', None, 'tp')
- mixed_moment: bfloat16 [8, 2560, 14336], P('rep', None, 'tp')
The draws below stay inside these ranges and needn't reach their ends.
All inputs are finite; a program needn't handle non-finite values.
Results may differ from the reference program's by a relative error of at most 0.0055.
Values may be sent and summed in bfloat16 or wider, within the bound.
A program may use at most 192 MiB of HBM per device.

```python
import jax
import jax.numpy as jnp

D = 2560
FF = 14336
TOK_DEV = 1536
REPLICAS = 8
TOKENS = 12288
N_REP = 8


def strengthened(entries, own_key, source, target, parts, factor):
    owner, partner = [(jnp.arange(entries.shape[dim]) // (entries.shape[dim] // parts)).reshape([-1 if axis == dim else 1 for axis in range(entries.ndim)]) for dim in (source, target)]
    chosen = jax.random.permutation(own_key, parts)[partner]
    strong = (owner == chosen) | (owner == (partner + parts // 2) % parts)
    return jnp.where(strong, factor * entries, entries)


def shard_levels(key, dims, shards, least, top_value):
    loudness = 1.0
    for axis_at, parts in shards:
        heights = jax.random.uniform(jax.random.fold_in(jax.random.fold_in(key, 6), axis_at), (parts,), jnp.float32, least / len(shards), top_value / len(shards))
        loudness = loudness * jnp.repeat(jnp.exp(heights), dims[axis_at] // parts).reshape((-1,) + (1,) * (len(dims) - 1 - axis_at))
    return loudness


def scatter_about(key, dims, spread, bound, pieces=(), dtype=jnp.bfloat16):
    drawn = spread * jax.random.normal(key, dims, jnp.float32)
    if pieces:
        drawn = drawn * shard_levels(key, dims, pieces, -0.22, 0.18)
    return jnp.clip(drawn, -bound, bound).astype(dtype)


def noise_with(key, dims, spread, limit, pieces, heavy, kind=jnp.bfloat16):
    entries = spread * jax.random.normal(key, dims, jnp.float32)
    if pieces:
        entries = entries * shard_levels(key, dims, pieces, -0.22, 0.18)
    return jnp.clip(strengthened(entries, jax.random.fold_in(key, 3), *heavy), -limit, limit).astype(kind)


def setup_inputs(seed: int = 0) -> dict:
    key_list = jax.random.split(jax.random.key(seed), 6)
    inputs = scatter_about(key_list[0], (TOKENS, D), 1.0, 6.0, ((0, 128),))
    gate_pre = scatter_about(key_list[1], (TOKENS, FF), 1.0, 6.0, ((0, 8), (1, 16)))
    grad_hidden = noise_with(key_list[2], (TOKENS, FF), 1.0, 6.0, ((0, 8), (1, 16)), (1, 0, 16, 2.0))
    up_weight = scatter_about(key_list[3], (REPLICAS, D, FF), 1.0, 6.0, ((0, 8), (2, 16)))
    momentum = scatter_about(key_list[4], (REPLICAS, D, FF), 0.5, 4.0, ((0, 8), (2, 16)))
    return dict(inputs=inputs, gate_pre=gate_pre, grad_hidden=grad_hidden, up_weight=up_weight, momentum=momentum)


momentum_beta = 0.9
learn_rate = 0.1


def reference(inputs, gate_pre, grad_hidden, up_weight, momentum):
    multiplier = D ** -0.5
    gate_act = jax.nn.silu(gate_pre.astype(jnp.float32))
    grad_up = (grad_hidden.astype(jnp.float32) * gate_act).astype(jnp.bfloat16)
    fresh_weights = []
    fresh_moments = []
    input_parts = []
    for replica in range(N_REP):
        tokens = inputs[replica * TOK_DEV:(replica + 1) * TOK_DEV]
        local_grad = grad_up[replica * TOK_DEV:(replica + 1) * TOK_DEV]
        weight_delta = jnp.dot(tokens.T, local_grad, preferred_element_type=jnp.float32) * multiplier
        input_part = jnp.dot(local_grad, up_weight[replica].T, preferred_element_type=jnp.float32) * multiplier
        input_parts.append(input_part.astype(jnp.bfloat16))
        fresh_moment = (momentum_beta * momentum[replica].astype(jnp.float32) + weight_delta).astype(jnp.bfloat16)
        fresh_weight = (up_weight[replica].astype(jnp.float32) - learn_rate * fresh_moment.astype(jnp.float32)).astype(jnp.bfloat16)
        fresh_weights.append(fresh_weight)
        fresh_moments.append(fresh_moment)
    mixed_weights = []
    mixed_moments = []
    for replica in range(N_REP):
        previous = (replica - 1) % N_REP
        following = (replica + 1) % N_REP
        mixed_weights.append(((fresh_weights[previous].astype(jnp.float32) + fresh_weights[replica].astype(jnp.float32) + fresh_weights[following].astype(jnp.float32)) / 3.0).astype(jnp.bfloat16))
        mixed_moments.append(((fresh_moments[previous].astype(jnp.float32) + fresh_moments[replica].astype(jnp.float32) + fresh_moments[following].astype(jnp.float32)) / 3.0).astype(jnp.bfloat16))
    return jnp.concatenate(input_parts, axis=0), jnp.stack(mixed_weights), jnp.stack(mixed_moments)
```

```python
import jax
import jax.numpy as jnp
from jax import lax
from jax.experimental import pallas as pl
from jax.experimental.pallas import tpu as pltpu
from jax.sharding import PartitionSpec as P

momentum_beta = 0.9
learn_rate = 0.1
CHUNK = 256
MESH = pl.DeviceIdType.MESH


def kernel(
    x_hbm, a_hbm, h_hbm, w_hbm, m_hbm,
    ig_hbm, mw_hbm, mm_hbm,
    wv, fv, g, xall, part, crecv, yrecv, xsend, xrecv, igv, wp, wn, fp, fn,
    loc, wsem_s, wsem_r, ag_s, ag_r, rs_s, rs_r, f_s, f_r, out_s,
):
    depth, width = wv.shape
    rows = x_hbm.shape[0]
    tokens = g.shape[0]
    chunks = depth // CHUNK
    scale = depth ** (-0.5)
    rep = lax.axis_index("rep")
    tp = lax.axis_index("tp")
    n_rep = lax.axis_size("rep")
    c = lax.rem(tp, 2)
    y = lax.rem(lax.div(tp, 2), 4)
    xl = lax.div(tp, 8)
    nxt = (lax.rem(rep + 1, n_rep), tp)
    prv = (lax.rem(rep + n_rep - 1, n_rep), tp)
    xother = (rep, tp + 8 - 16 * xl)
    cother = (rep, tp + 1 - 2 * c)
    yo = [lax.rem(y + k, 4) for k in (1, 2, 3)]
    yother = [(rep, xl * 8 + yk * 2 + c) for yk in yo]

    def remote(src, dst, s, r, dev):
        return pltpu.make_async_remote_copy(
            src_ref=src, dst_ref=dst, send_sem=s, recv_sem=r, device_id=dev, device_id_type=MESH
        )

    load_a = pltpu.make_async_copy(a_hbm, fv.at[pl.ds(0, tokens)], loc.at[0])
    load_h = pltpu.make_async_copy(h_hbm, g, loc.at[1])
    load_w = pltpu.make_async_copy(w_hbm, wv, loc.at[2])
    load_x = pltpu.make_async_copy(x_hbm, xall.at[xl, y, c], loc.at[3])
    load_m = pltpu.make_async_copy(m_hbm, fv, loc.at[4])
    load_a.start()
    load_h.start()
    load_w.start()
    load_x.start()

    barrier = pltpu.get_barrier_semaphore()
    for dev in [nxt, prv, xother, cother] + yother:
        pl.semaphore_signal(barrier, inc=1, device_id=dev, device_id_type=MESH)
    pl.semaphore_wait(barrier, 7)

    own = xall.at[xl, y, c]
    ag_x = remote(x_hbm, own, ag_s.at[0], ag_r.at[0], xother)
    ag_y0 = [remote(x_hbm, own, ag_s.at[1 + k], ag_r.at[1 + k], yother[k]) for k in range(3)]
    ag_x.start()
    for cp in ag_y0:
        cp.start()
    w_next = remote(w_hbm, wp, wsem_s.at[0], wsem_r.at[0], nxt)
    w_prev = remote(w_hbm, wn, wsem_s.at[1], wsem_r.at[1], prv)
    w_next.start()
    w_prev.start()

    load_a.wait()
    load_h.wait()

    def act(i, _):
        blk = pl.ds(i * 64, 64)
        v = fv[blk].astype(jnp.float32)
        g[blk] = (g[blk].astype(jnp.float32) * (v / (1.0 + jnp.exp(-v)))).astype(jnp.bfloat16)
        return 0

    lax.fori_loop(0, tokens // 64, act, 0)
    load_m.start()

    far = xall.at[1 - xl, y, c]
    ag_x.wait_recv()
    ag_y1 = [remote(far, far, ag_s.at[4 + k], ag_r.at[4 + k], yother[k]) for k in range(3)]
    for cp in ag_y1:
        cp.start()

    load_w.wait()

    def cot(n, _):
        cols = pl.ds(pl.multiple_of(n * CHUNK, CHUNK), CHUNK)
        res = lax.dot_general(
            g[...], wv[cols], (((1,), (1,)), ((), ())), preferred_element_type=jnp.float32
        )
        part[:, :, :, cols] = res.astype(jnp.bfloat16).reshape(8, 2, rows, CHUNK)
        return 0

    lax.fori_loop(0, chunks, cot, 0)
    rs_c = remote(part.at[:, 1 - c], crecv, rs_s.at[0], rs_r.at[0], cother)

    load_x.wait()
    for cp in ag_y0:
        cp.wait_recv()
    ag_c0 = remote(xall.at[xl, :, c], xall.at[xl, :, c], ag_s.at[7], ag_r.at[7], cother)
    ag_c0.start()
    rs_c.start()
    for cp in ag_y1:
        cp.wait_recv()
    ag_c1 = remote(xall.at[1 - xl, :, c], xall.at[1 - xl, :, c], ag_s.at[8], ag_r.at[8], cother)
    ag_c1.start()

    rs_c.wait_recv()

    def add_core(b, _):
        u, v = lax.div(b, 4), lax.rem(b, 4)
        crecv[b] = (part[b, c].astype(jnp.float32) + crecv[b].astype(jnp.float32)).astype(jnp.bfloat16)
        return 0

    lax.fori_loop(0, 8, add_core, 0)
    rs_y = []
    for k in range(3):
        for u in range(2):
            j = 1 + 2 * k + u
            rs_y.append(
                remote(crecv.at[4 * u + yo[k]], yrecv.at[k, u], rs_s.at[j], rs_r.at[j], yother[k])
            )
    for cp in rs_y:
        cp.start()

    ag_c0.wait_recv()
    ag_c1.wait_recv()
    load_m.wait()

    def moment(n, _):
        blk = pl.ds(pl.multiple_of(n * CHUNK, CHUNK), CHUNK)
        xs = xall[:, :, :, :, blk].reshape(tokens, CHUNK)
        delta = lax.dot_general(
            xs, g[...], (((0,), (0,)), ((), ())), preferred_element_type=jnp.float32
        )
        fv[blk] = (momentum_beta * fv[blk].astype(jnp.float32) + delta * scale).astype(jnp.bfloat16)
        remote(fv.at[blk], fp.at[blk], f_s.at[0, n], f_r.at[0, n], nxt).start()
        remote(fv.at[blk], fn.at[blk], f_s.at[1, n], f_r.at[1, n], prv).start()
        return 0

    lax.fori_loop(0, chunks, moment, 0)

    for cp in rs_y:
        cp.wait_recv()

    def over_y(u):
        return (
            crecv[4 * u + y].astype(jnp.float32)
            + yrecv[0, u].astype(jnp.float32)
            + yrecv[1, u].astype(jnp.float32)
            + yrecv[2, u].astype(jnp.float32)
        )

    xsend[...] = over_y(1 - xl).astype(jnp.bfloat16)
    rs_x = remote(xsend, xrecv, rs_s.at[7], rs_r.at[7], xother)
    rs_x.start()
    rs_x.wait_recv()
    igv[...] = ((over_y(xl) + xrecv[...].astype(jnp.float32)) * scale).astype(jnp.bfloat16)
    out_ig = pltpu.make_async_copy(igv, ig_hbm, loc.at[5])
    out_ig.start()

    w_next.wait_recv()
    w_prev.wait_recv()

    def fresh(w, f):
        return (w.astype(jnp.float32) - learn_rate * f).astype(jnp.bfloat16).astype(jnp.float32)

    def mix(n, _):
        blk = pl.ds(pl.multiple_of(n * CHUNK, CHUNK), CHUNK)
        remote(fv.at[blk], fp.at[blk], f_s.at[0, n], f_r.at[0, n], nxt).wait()
        remote(fv.at[blk], fn.at[blk], f_s.at[1, n], f_r.at[1, n], prv).wait()

        def piece(i, _):
            sub = pl.ds(pl.multiple_of(n * CHUNK + i * 32, 32), 32)
            f0, f1, f2 = (r[sub].astype(jnp.float32) for r in (fp, fv, fn))
            w = fresh(wp[sub], f0) + fresh(wv[sub], f1) + fresh(wn[sub], f2)
            wp[sub] = (w / 3.0).astype(jnp.bfloat16)
            fp[sub] = ((f0 + f1 + f2) / 3.0).astype(jnp.bfloat16)
            return 0

        lax.fori_loop(0, CHUNK // 32, piece, 0)
        pltpu.make_async_copy(wp.at[blk], mw_hbm.at[blk], out_s.at[0, n]).start()
        pltpu.make_async_copy(fp.at[blk], mm_hbm.at[blk], out_s.at[1, n]).start()
        return 0

    lax.fori_loop(0, chunks, mix, 0)

    def drain(n, _):
        blk = pl.ds(pl.multiple_of(n * CHUNK, CHUNK), CHUNK)
        pltpu.make_async_copy(wp.at[blk], mw_hbm.at[blk], out_s.at[0, n]).wait()
        pltpu.make_async_copy(fp.at[blk], mm_hbm.at[blk], out_s.at[1, n]).wait()
        return 0

    lax.fori_loop(0, chunks, drain, 0)
    out_ig.wait()
    for cp in [ag_x, *ag_y0, *ag_y1, ag_c0, ag_c1, rs_c, *rs_y, rs_x, w_next, w_prev]:
        cp.wait_send()


def per_device(inputs, gate_pre, grad_hidden, up_weight, momentum):
    rows, depth = inputs.shape
    tokens, width = gate_pre.shape
    chunks = depth // CHUNK
    bf = jnp.bfloat16
    any_spec = pl.BlockSpec(memory_space=pl.ANY)
    dma = pltpu.SemaphoreType.DMA
    big = pltpu.VMEM((depth, width), bf)
    ig, mw, mm = pl.pallas_call(
        kernel,
        out_shape=(
            jax.ShapeDtypeStruct((rows, depth), bf),
            jax.ShapeDtypeStruct((depth, width), bf),
            jax.ShapeDtypeStruct((depth, width), bf),
        ),
        in_specs=[any_spec] * 5,
        out_specs=(any_spec,) * 3,
        scratch_shapes=[
            big,
            big,
            pltpu.VMEM((tokens, width), bf),
            pltpu.VMEM((2, 4, 2, rows, depth), bf),
            pltpu.VMEM((8, 2, rows, depth), bf),
            pltpu.VMEM((8, rows, depth), bf),
            pltpu.VMEM((3, 2, rows, depth), bf),
            pltpu.VMEM((rows, depth), bf),
            pltpu.VMEM((rows, depth), bf),
            pltpu.VMEM((rows, depth), bf),
            big,
            big,
            big,
            big,
            dma((6,)),
            dma((2,)),
            dma((2,)),
            dma((9,)),
            dma((9,)),
            dma((8,)),
            dma((8,)),
            dma((2, chunks)),
            dma((2, chunks)),
            dma((2, chunks)),
        ],
        compiler_params=pltpu.CompilerParams(
            collective_id=0, has_side_effects=True, vmem_limit_bytes=62 * 2**20
        ),
        name="step",
    )(inputs, gate_pre, grad_hidden, up_weight[0], momentum[0])
    return ig, mw[None], mm[None]


def solution(mesh):
    in_specs = (
        P(("rep", "tp"), None),
        P("rep", "tp"),
        P("rep", "tp"),
        P("rep", None, "tp"),
        P("rep", None, "tp"),
    )
    out_specs = (P(("rep", "tp"), None), P("rep", None, "tp"), P("rep", None, "tp"))
    return jax.shard_map(
        per_device, mesh=mesh, in_specs=in_specs, out_specs=out_specs, check_vma=False
    )
```

```python
import jax
import jax.numpy as jnp
from jax import lax
from jax.experimental import pallas as pl
from jax.experimental.pallas import tpu as pltpu
from jax.sharding import PartitionSpec as P

momentum_beta = 0.9
learn_rate = 0.1
CHUNK = 256
INNER_ROWS = 512
OUTER_ROWS = 320
PIECE = 32
FIRST = 4
LATE = 7
MESH = pl.DeviceIdType.MESH


def kernel(
    x_hbm, a_hbm, h_hbm, w_hbm, m_hbm,
    ig_hbm, mw_hbm, mm_hbm,
    wv, fv, g, xall, part, crecv, yrecv, xsend, xrecv, igv, wn, wo, fn, fo,
    relw,
    loc, wsem_s, wsem_r, ag_s, ag_r, rs_s, rs_r, f_s, f_r, rel_s, rel_r, out_s,
):
    depth, width = wv.shape
    rows = x_hbm.shape[0]
    tokens = g.shape[0]
    chunks = depth // CHUNK
    scale = depth ** (-0.5)
    rep = lax.axis_index("rep")
    tp = lax.axis_index("tp")
    c = lax.rem(tp, 2)
    y = lax.rem(lax.div(tp, 2), 4)
    xl = lax.div(tp, 8)
    yo = [lax.rem(y + k, 4) for k in (1, 2, 3)]
    yother = [(rep, xl * 8 + yk * 2 + c) for yk in yo]
    odd = lax.rem(rep, 2)
    quad = lax.rem(rep, 4)
    inner = jnp.logical_or(quad == 1, quad == 2)
    near = (rep + 1 - 2 * odd, tp)
    out = (lax.rem(rep + 7 + 2 * odd, 8), tp)
    across = (jnp.where(inner, 7 - rep, 3 - rep + 8 * lax.div(rep, 4)), tp)
    xother = (rep, tp + 8 - 16 * xl)
    cother = (rep, tp + 1 - 2 * c)
    inner_rows = pl.ds(0, INNER_ROWS)
    outer_rows = pl.ds(INNER_ROWS, OUTER_ROWS)
    rest = pl.ds(INNER_ROWS + OUTER_ROWS, depth - INNER_ROWS - OUTER_ROWS)

    def by_kind(run):
        pl.when(inner)(lambda: run(inner_rows, outer_rows))
        pl.when(jnp.logical_not(inner))(lambda: run(outer_rows, inner_rows))

    def remote(src, dst, s, r, dev):
        return pltpu.make_async_remote_copy(
            src_ref=src, dst_ref=dst, send_sem=s, recv_sem=r, device_id=dev, device_id_type=MESH
        )

    load_a = pltpu.make_async_copy(a_hbm, fv.at[pl.ds(0, tokens)], loc.at[0])
    load_h = pltpu.make_async_copy(h_hbm, g, loc.at[1])
    load_w = pltpu.make_async_copy(w_hbm, wv, loc.at[2])
    load_x = pltpu.make_async_copy(x_hbm, xall.at[xl, y, c], loc.at[3])
    load_m = pltpu.make_async_copy(m_hbm, fv, loc.at[4])
    load_a.start()
    load_h.start()
    load_w.start()
    load_x.start()

    barrier = pltpu.get_barrier_semaphore()
    for dev in [near, out, across, xother, cother] + yother:
        pl.semaphore_signal(barrier, inc=1, device_id=dev, device_id_type=MESH)
    pl.semaphore_wait(barrier, 8)

    own = xall.at[xl, y, c]
    ag_x = remote(x_hbm, own, ag_s.at[0], ag_r.at[0], xother)
    ag_y0 = [remote(x_hbm, own, ag_s.at[1 + k], ag_r.at[1 + k], yother[k]) for k in range(3)]
    ag_x.start()
    for cp in ag_y0:
        cp.start()
    w_near = remote(w_hbm.at[rest], wn.at[rest], wsem_s.at[0, 1], wsem_r.at[0, 1], near)
    w_out = remote(w_hbm.at[rest], wo.at[rest], wsem_s.at[1, 1], wsem_r.at[1, 1], out)

    def near_rows(blk):
        return remote(w_hbm.at[blk], wn.at[blk], wsem_s.at[0, 0], wsem_r.at[0, 0], near)

    def out_rows(blk):
        return remote(w_hbm.at[blk], wo.at[blk], wsem_s.at[1, 0], wsem_r.at[1, 0], out)

    def relay(blk):
        return remote(wn.at[blk], relw.at[pl.ds(0, blk.size)], rel_s.at[0], rel_r.at[0], across)

    def sums(blk):
        return remote(relw.at[pl.ds(0, blk.size)], wn.at[blk], rel_s.at[1], rel_r.at[1], near)

    def first_rows(mine, theirs):
        near_rows(theirs).start()
        out_rows(mine).start()

    by_kind(first_rows)
    w_near.start()
    w_out.start()

    load_a.wait()
    load_h.wait()

    def act(i, _):
        blk = pl.ds(i * 64, 64)
        v = fv[blk].astype(jnp.float32)
        g[blk] = (g[blk].astype(jnp.float32) * (v / (1.0 + jnp.exp(-v)))).astype(jnp.bfloat16)
        return 0

    lax.fori_loop(0, tokens // 64, act, 0)
    load_m.start()

    far = xall.at[1 - xl, y, c]
    ag_x.wait_recv()
    ag_y1 = [remote(far, far, ag_s.at[4 + k], ag_r.at[4 + k], yother[k]) for k in range(3)]
    for cp in ag_y1:
        cp.start()

    load_w.wait()

    def cot(n, _):
        cols = pl.ds(pl.multiple_of(n * CHUNK, CHUNK), CHUNK)
        res = lax.dot_general(
            g[...], wv[cols], (((1,), (1,)), ((), ())), preferred_element_type=jnp.float32
        )
        part[:, :, :, cols] = res.astype(jnp.bfloat16).reshape(8, 2, rows, CHUNK)
        return 0

    lax.fori_loop(0, chunks, cot, 0)

    def pass_on(mine, theirs):
        near_rows(mine).wait_recv()
        relay(mine).start()

    by_kind(pass_on)
    rs_c = remote(part.at[:, 1 - c], crecv, rs_s.at[0], rs_r.at[0], cother)

    load_x.wait()
    for cp in ag_y0:
        cp.wait_recv()
    ag_c0 = remote(xall.at[xl, :, c], xall.at[xl, :, c], ag_s.at[7], ag_r.at[7], cother)
    ag_c0.start()
    rs_c.start()
    for cp in ag_y1:
        cp.wait_recv()
    ag_c1 = remote(xall.at[1 - xl, :, c], xall.at[1 - xl, :, c], ag_s.at[8], ag_r.at[8], cother)
    ag_c1.start()

    rs_c.wait_recv()

    def add_core(b, _):
        u, v = lax.div(b, 4), lax.rem(b, 4)
        crecv[b] = (part[b, c].astype(jnp.float32) + crecv[b].astype(jnp.float32)).astype(jnp.bfloat16)
        return 0

    lax.fori_loop(0, 8, add_core, 0)
    rs_y = []
    for k in range(3):
        for u in range(2):
            j = 1 + 2 * k + u
            rs_y.append(
                remote(crecv.at[4 * u + yo[k]], yrecv.at[k, u], rs_s.at[j], rs_r.at[j], yother[k])
            )
    for cp in rs_y:
        cp.start()

    ag_c0.wait_recv()
    ag_c1.wait_recv()
    load_m.wait()

    def send_near(blk, n):
        return remote(fv.at[blk], fn.at[blk], f_s.at[0, n], f_r.at[0, n], near)

    def send_out(blk, n):
        return remote(fv.at[blk], fo.at[blk], f_s.at[1, n], f_r.at[1, n], out)

    def moment(blk):
        xs = xall[:, :, :, :, blk].reshape(tokens, CHUNK)
        delta = lax.dot_general(
            xs, g[...], (((0,), (0,)), ((), ())), preferred_element_type=jnp.float32
        )
        fv[blk] = (momentum_beta * fv[blk].astype(jnp.float32) + delta * scale).astype(jnp.bfloat16)

    def rows_of(n):
        return pl.ds(pl.multiple_of(n * CHUNK, CHUNK), CHUNK)

    def moments(n, _):
        moment(rows_of(n))
        return 0

    def send(lo, hi, *ways):
        def go(n, _):
            for way in ways:
                way(rows_of(n), n).start()
            return 0

        lax.fori_loop(lo, hi, go, 0)

    def early(n, _):
        moments(n, 0)
        send_near(rows_of(n), n).start()
        pl.when(inner)(lambda: send_out(rows_of(n), n).start())
        return 0

    lax.fori_loop(0, FIRST, early, 0)
    lax.fori_loop(FIRST, chunks, moments, 0)

    def send_sum(mine, theirs):
        relay(mine).wait_recv()

        def add_own(i, _):
            here = pl.ds(pl.multiple_of(i * PIECE, PIECE), PIECE)
            sub = pl.ds(pl.multiple_of(mine.start + i * PIECE, PIECE), PIECE)
            relw[here] = (relw[here].astype(jnp.float32) + wv[sub].astype(jnp.float32)).astype(jnp.bfloat16)
            return 0

        lax.fori_loop(0, mine.size // PIECE, add_own, 0)
        sums(mine).start()

    pl.when(inner)(lambda: send_sum(inner_rows, outer_rows))

    for cp in rs_y:
        cp.wait_recv()

    def over_y(u):
        return (
            crecv[4 * u + y].astype(jnp.float32)
            + yrecv[0, u].astype(jnp.float32)
            + yrecv[1, u].astype(jnp.float32)
            + yrecv[2, u].astype(jnp.float32)
        )

    xsend[...] = over_y(1 - xl).astype(jnp.bfloat16)
    rs_x = remote(xsend, xrecv, rs_s.at[7], rs_r.at[7], xother)
    rs_x.start()
    pl.when(inner)(lambda: send(FIRST, chunks, send_near, send_out))

    @pl.when(jnp.logical_not(inner))
    def _():
        relay(outer_rows).wait_send()
        send(0, chunks, send_out)
        send_sum(outer_rows, inner_rows)
        send(FIRST, chunks, send_near)

    w_near.wait_recv()
    w_out.wait_recv()

    def last_rows(mine, theirs):
        out_rows(mine).wait_recv()
        sums(theirs).wait_recv()

    by_kind(last_rows)
    pl.when(inner)(lambda: relay(inner_rows).wait_send())
    low = jnp.where(inner, INNER_ROWS, 0)
    high = jnp.where(inner, INNER_ROWS + OUTER_ROWS, INNER_ROWS)

    def fresh(w, f):
        return (w.astype(jnp.float32) - learn_rate * f).astype(jnp.bfloat16).astype(jnp.float32)

    def outputs(n):
        blk = rows_of(n)
        return (
            pltpu.make_async_copy(wn.at[blk], mw_hbm.at[blk], out_s.at[0, n]),
            pltpu.make_async_copy(fn.at[blk], mm_hbm.at[blk], out_s.at[1, n]),
        )

    def mix(n, _):
        blk = rows_of(n)
        send_near(blk, n).wait_recv()
        send_out(blk, n).wait_recv()

        def piece(i, _):
            start = n * CHUNK + i * PIECE
            sub = pl.ds(pl.multiple_of(start, PIECE), PIECE)
            summed = jnp.logical_and(start >= low, start < high)
            f0, f1, f2 = (r[sub].astype(jnp.float32) for r in (fn, fv, fo))
            own = fresh(wv[sub], f1)

            @pl.when(summed)
            def _():
                w = wn[sub].astype(jnp.float32) - learn_rate * (f0 + f2) + own
                wn[sub] = (w * (1.0 / 3.0)).astype(jnp.bfloat16)

            @pl.when(jnp.logical_not(summed))
            def _():
                w = fresh(wn[sub], f0) + own + fresh(wo[sub], f2)
                wn[sub] = (w * (1.0 / 3.0)).astype(jnp.bfloat16)

            fn[sub] = ((f0 + f1 + f2) * (1.0 / 3.0)).astype(jnp.bfloat16)
            return 0

        lax.fori_loop(0, CHUNK // PIECE, piece, 0)
        for cp in outputs(n):
            cp.start()
        return 0

    lax.fori_loop(0, LATE, mix, 0)
    rs_x.wait_recv()
    igv[...] = ((over_y(xl) + xrecv[...].astype(jnp.float32)) * scale).astype(jnp.bfloat16)
    out_ig = pltpu.make_async_copy(igv, ig_hbm, loc.at[5])
    out_ig.start()
    lax.fori_loop(LATE, chunks, mix, 0)

    def drain(n, _):
        blk = rows_of(n)
        send_near(blk, n).wait_send()
        send_out(blk, n).wait_send()
        for cp in outputs(n):
            cp.wait()
        return 0

    lax.fori_loop(0, chunks, drain, 0)
    out_ig.wait()
    def sent(mine, theirs):
        near_rows(theirs).wait_send()
        out_rows(mine).wait_send()
        sums(mine).wait_send()

    by_kind(sent)
    for cp in [ag_x, *ag_y0, *ag_y1, ag_c0, ag_c1, rs_c, *rs_y, rs_x, w_near, w_out]:
        cp.wait_send()


def per_device(inputs, gate_pre, grad_hidden, up_weight, momentum):
    rows, depth = inputs.shape
    tokens, width = gate_pre.shape
    chunks = depth // CHUNK
    bf = jnp.bfloat16
    any_spec = pl.BlockSpec(memory_space=pl.ANY)
    dma = pltpu.SemaphoreType.DMA
    big = pltpu.VMEM((depth, width), bf)
    ig, mw, mm = pl.pallas_call(
        kernel,
        out_shape=(
            jax.ShapeDtypeStruct((rows, depth), bf),
            jax.ShapeDtypeStruct((depth, width), bf),
            jax.ShapeDtypeStruct((depth, width), bf),
        ),
        in_specs=[any_spec] * 5,
        out_specs=(any_spec,) * 3,
        scratch_shapes=[
            big,
            big,
            pltpu.VMEM((tokens, width), bf),
            pltpu.VMEM((2, 4, 2, rows, depth), bf),
            pltpu.VMEM((8, 2, rows, depth), bf),
            pltpu.VMEM((8, rows, depth), bf),
            pltpu.VMEM((3, 2, rows, depth), bf),
            pltpu.VMEM((rows, depth), bf),
            pltpu.VMEM((rows, depth), bf),
            pltpu.VMEM((rows, depth), bf),
            big,
            big,
            big,
            big,
            pltpu.VMEM((max(INNER_ROWS, OUTER_ROWS), width), bf),
            dma((6,)),
            dma((2, 2)),
            dma((2, 2)),
            dma((9,)),
            dma((9,)),
            dma((8,)),
            dma((8,)),
            dma((2, chunks)),
            dma((2, chunks)),
            dma((2,)),
            dma((2,)),
            dma((2, chunks)),
        ],
        compiler_params=pltpu.CompilerParams(
            collective_id=0, has_side_effects=True, vmem_limit_bytes=62 * 2**20
        ),
        name="step",
    )(inputs, gate_pre, grad_hidden, up_weight[0], momentum[0])
    return ig, mw[None], mm[None]


def solution(mesh):
    in_specs = (
        P(("rep", "tp"), None),
        P("rep", "tp"),
        P("rep", "tp"),
        P("rep", None, "tp"),
        P("rep", None, "tp"),
    )
    out_specs = (P(("rep", "tp"), None), P("rep", None, "tp"), P("rep", None, "tp"))
    return jax.shard_map(
        per_device, mesh=mesh, in_specs=in_specs, out_specs=out_specs, check_vma=False
    )
```

```python
import jax
import jax.numpy as jnp
from jax import lax
from jax.experimental import pallas as pl
from jax.experimental.pallas import tpu as pltpu
from jax.sharding import PartitionSpec as P

momentum_beta = 0.9
learn_rate = 0.1
CHUNK = 256
INNER_ROWS = (640,)
OUTER_ROWS = (288, 320)
PIECE = 32
FIRST = 4
LATE = 7
MESH = pl.DeviceIdType.MESH


def kernel(
    x_hbm, a_hbm, h_hbm, w_hbm, m_hbm,
    igv, wn, fn,
    wv, fv, g, xall, part, crecv, yrecv, xsend, xrecv, wo, fo,
    relw,
    loc, wsem_s, wsem_r, ag_s, ag_r, rs_s, rs_r, f_s, f_r, rel_s, rel_r, grants,
):
    depth, width = wv.shape
    rows = x_hbm.shape[0]
    tokens = g.shape[0]
    chunks = depth // CHUNK
    scale = depth ** (-0.5)
    rep = lax.axis_index("rep")
    tp = lax.axis_index("tp")
    c = lax.rem(tp, 2)
    y = lax.rem(lax.div(tp, 2), 4)
    xl = lax.div(tp, 8)
    yo = [lax.rem(y + k, 4) for k in (1, 2, 3)]
    yother = [(rep, xl * 8 + yk * 2 + c) for yk in yo]
    odd = lax.rem(rep, 2)
    quad = lax.rem(rep, 4)
    inner = jnp.logical_or(quad == 1, quad == 2)
    near = (rep + 1 - 2 * odd, tp)
    out = (lax.rem(rep + 7 + 2 * odd, 8), tp)
    across = (jnp.where(inner, 7 - rep, 3 - rep + 8 * lax.div(rep, 4)), tp)
    xother = (rep, tp + 8 - 16 * xl)
    cother = (rep, tp + 1 - 2 * c)
    outs = (out, (out[0], cother[1]))
    inner_rows, outer_rows, at = [], [], 0
    for sizes, blocks in ((INNER_ROWS, inner_rows), (OUTER_ROWS, outer_rows)):
        for size in sizes:
            blocks.append(pl.ds(at, size))
            at += size
    rest = pl.ds(at, depth - at)

    def by_kind(run):
        pl.when(inner)(lambda: run(inner_rows, outer_rows))
        pl.when(jnp.logical_not(inner))(lambda: run(outer_rows, inner_rows))

    def remote(src, dst, s, r, dev):
        return pltpu.make_async_remote_copy(
            src_ref=src, dst_ref=dst, send_sem=s, recv_sem=r, device_id=dev, device_id_type=MESH
        )

    load_a = pltpu.make_async_copy(a_hbm, fv.at[pl.ds(0, tokens)], loc.at[0])
    load_h = pltpu.make_async_copy(h_hbm, g, loc.at[1])
    load_w = pltpu.make_async_copy(w_hbm, wv, loc.at[2])
    load_x = pltpu.make_async_copy(x_hbm, xall.at[xl, y, c], loc.at[3])
    load_m = pltpu.make_async_copy(m_hbm, fv, loc.at[4])
    load_a.start()
    load_h.start()
    load_w.start()
    load_x.start()

    barrier = pltpu.get_barrier_semaphore()
    for dev in [near, *outs, across, xother, cother] + yother:
        pl.semaphore_signal(barrier, inc=1, device_id=dev, device_id_type=MESH)
    pl.semaphore_wait(barrier, 9)

    own = xall.at[xl, y, c]
    ag_x = remote(x_hbm, own, ag_s.at[0], ag_r.at[0], xother)
    ag_y0 = [remote(x_hbm, own, ag_s.at[1 + k], ag_r.at[1 + k], yother[k]) for k in range(3)]
    w_near = remote(w_hbm.at[rest], wn.at[rest], wsem_s.at[0, 2], wsem_r.at[0, 2], near)
    w_out = remote(w_hbm.at[rest], wo.at[rest], wsem_s.at[1, 2], wsem_r.at[1, 2], out)

    def near_rows(blocks):
        return [
            remote(w_hbm.at[blk], wn.at[blk], wsem_s.at[0, i], wsem_r.at[0, i], near)
            for i, blk in enumerate(blocks)
        ]

    def out_rows(blocks):
        return [
            remote(w_hbm.at[blk], wo.at[blk], wsem_s.at[1, i], wsem_r.at[1, i], out)
            for i, blk in enumerate(blocks)
        ]

    def relays(blocks):
        return [
            remote(
                wn.at[blk],
                relw.at[pl.ds(blk.start - blocks[0].start, blk.size)],
                rel_s.at[i],
                rel_r.at[i],
                across,
            )
            for i, blk in enumerate(blocks)
        ]

    def sums(blocks):
        size = sum(blk.size for blk in blocks)
        return remote(
            relw.at[pl.ds(0, size)],
            wn.at[pl.ds(blocks[0].start, size)],
            rel_s.at[2],
            rel_r.at[2],
            near,
        )

    def pass_on(blocks, i):
        near_rows(blocks)[i].wait_recv()
        relays(blocks)[i].start()

    def granted(i):
        relays(outer_rows)[i].wait_recv()
        for dev in outs:
            pl.semaphore_signal(grants.at[i], inc=1, device_id=dev, device_id_type=MESH)
        pl.semaphore_wait(grants.at[i], 2)

    for cp in ag_y0:
        cp.start()

    @pl.when(inner)
    def _():
        ag_x.start()
        for cp in near_rows(outer_rows) + out_rows(inner_rows) + [w_near, w_out]:
            cp.start()

    @pl.when(jnp.logical_not(inner))
    def _():
        out_rows(outer_rows)[0].start()
        ag_x.start()
        for cp in near_rows(inner_rows) + [w_near]:
            cp.start()

    load_a.wait()
    load_h.wait()

    def act(i, _):
        blk = pl.ds(i * 64, 64)
        v = fv[blk].astype(jnp.float32)
        g[blk] = (g[blk].astype(jnp.float32) * (v / (1.0 + jnp.exp(-v)))).astype(jnp.bfloat16)
        return 0

    lax.fori_loop(0, tokens // 64, act, 0)
    load_m.start()

    pl.when(jnp.logical_not(inner))(lambda: pass_on(outer_rows, 0))

    load_w.wait()

    def cot(n, _):
        cols = pl.ds(pl.multiple_of(n * CHUNK, CHUNK), CHUNK)
        res = lax.dot_general(
            g[...], wv[cols], (((1,), (1,)), ((), ())), preferred_element_type=jnp.float32
        )
        part[:, :, :, cols] = res.astype(jnp.bfloat16).reshape(8, 2, rows, CHUNK)
        return 0

    lax.fori_loop(0, chunks, cot, 0)

    far = xall.at[1 - xl, y, c]
    ag_x.wait_recv()
    ag_y1 = [remote(far, far, ag_s.at[4 + k], ag_r.at[4 + k], yother[k]) for k in range(3)]
    for cp in ag_y1:
        cp.start()

    pl.when(inner)(lambda: pass_on(inner_rows, 0))

    @pl.when(jnp.logical_not(inner))
    def _():
        relays(outer_rows)[0].wait_send()
        out_rows(outer_rows)[1].start()
        pass_on(outer_rows, 1)
        granted(0)
        w_out.start()

    rs_c = remote(part.at[:, 1 - c], crecv, rs_s.at[0], rs_r.at[0], cother)

    load_x.wait()
    for cp in ag_y0:
        cp.wait_recv()
    ag_c0 = remote(xall.at[xl, :, c], xall.at[xl, :, c], ag_s.at[7], ag_r.at[7], cother)
    ag_c0.start()
    rs_c.start()
    for cp in ag_y1:
        cp.wait_recv()
    ag_c1 = remote(xall.at[1 - xl, :, c], xall.at[1 - xl, :, c], ag_s.at[8], ag_r.at[8], cother)
    ag_c1.start()

    rs_c.wait_recv()

    def add_core(b, _):
        u, v = lax.div(b, 4), lax.rem(b, 4)
        crecv[b] = (part[b, c].astype(jnp.float32) + crecv[b].astype(jnp.float32)).astype(jnp.bfloat16)
        return 0

    lax.fori_loop(0, 8, add_core, 0)
    rs_y = []
    for k in range(3):
        for u in range(2):
            j = 1 + 2 * k + u
            rs_y.append(
                remote(crecv.at[4 * u + yo[k]], yrecv.at[k, u], rs_s.at[j], rs_r.at[j], yother[k])
            )
    for cp in rs_y:
        cp.start()

    ag_c0.wait_recv()
    ag_c1.wait_recv()
    load_m.wait()

    def send_near(blk, n):
        return remote(fv.at[blk], fn.at[blk], f_s.at[0, n], f_r.at[0, n], near)

    def send_out(blk, n):
        return remote(fv.at[blk], fo.at[blk], f_s.at[1, n], f_r.at[1, n], out)

    def moment(blk):
        xs = xall[:, :, :, :, blk].reshape(tokens, CHUNK)
        delta = lax.dot_general(
            xs, g[...], (((0,), (0,)), ((), ())), preferred_element_type=jnp.float32
        )
        fv[blk] = (momentum_beta * fv[blk].astype(jnp.float32) + delta * scale).astype(jnp.bfloat16)

    def rows_of(n):
        return pl.ds(pl.multiple_of(n * CHUNK, CHUNK), CHUNK)

    def moments(n, _):
        moment(rows_of(n))
        return 0

    def send(lo, hi, *ways):
        def go(n, _):
            for way in ways:
                way(rows_of(n), n).start()
            return 0

        lax.fori_loop(lo, hi, go, 0)

    def early(n, _):
        moments(n, 0)
        send_near(rows_of(n), n).start()
        pl.when(inner)(lambda: send_out(rows_of(n), n).start())
        return 0

    lax.fori_loop(0, FIRST, early, 0)
    lax.fori_loop(FIRST, chunks, moments, 0)

    def send_sum(mine):
        size = sum(blk.size for blk in mine)

        def add_own(i, _):
            here = pl.ds(pl.multiple_of(i * PIECE, PIECE), PIECE)
            sub = pl.ds(pl.multiple_of(mine[0].start + i * PIECE, PIECE), PIECE)
            relw[here] = (relw[here].astype(jnp.float32) + wv[sub].astype(jnp.float32)).astype(jnp.bfloat16)
            return 0

        lax.fori_loop(0, size // PIECE, add_own, 0)
        sums(mine).start()

    @pl.when(inner)
    def _():
        relays(inner_rows)[0].wait_recv()
        send_sum(inner_rows)

    for cp in rs_y:
        cp.wait_recv()

    def over_y(u):
        return (
            crecv[4 * u + y].astype(jnp.float32)
            + yrecv[0, u].astype(jnp.float32)
            + yrecv[1, u].astype(jnp.float32)
            + yrecv[2, u].astype(jnp.float32)
        )

    xsend[...] = over_y(1 - xl).astype(jnp.bfloat16)
    rs_x = remote(xsend, xrecv, rs_s.at[7], rs_r.at[7], xother)
    rs_x.start()
    pl.when(inner)(lambda: send(FIRST, chunks, send_near, send_out))

    @pl.when(jnp.logical_not(inner))
    def _():
        relays(outer_rows)[1].wait_send()
        send(0, 1, send_out)
        granted(1)
        send(1, chunks, send_out)
        send_sum(outer_rows)
        send(FIRST, chunks, send_near)

    w_near.wait_recv()
    w_out.wait_recv()

    def last_rows(mine, theirs):
        for cp in out_rows(mine):
            cp.wait_recv()
        sums(theirs).wait_recv()

    by_kind(last_rows)
    pl.when(inner)(lambda: relays(inner_rows)[0].wait_send())
    low = jnp.where(inner, outer_rows[0].start, 0)
    high = jnp.where(inner, rest.start, outer_rows[0].start)

    def fresh(w, f):
        return (w.astype(jnp.float32) - learn_rate * f).astype(jnp.bfloat16).astype(jnp.float32)

    def mix(n, _):
        blk = rows_of(n)
        send_near(blk, n).wait_recv()
        send_out(blk, n).wait_recv()

        def piece(i, _):
            start = n * CHUNK + i * PIECE
            sub = pl.ds(pl.multiple_of(start, PIECE), PIECE)
            summed = jnp.logical_and(start >= low, start < high)
            f0, f1, f2 = (r[sub].astype(jnp.float32) for r in (fn, fv, fo))
            own = fresh(wv[sub], f1)

            @pl.when(summed)
            def _():
                w = wn[sub].astype(jnp.float32) - learn_rate * (f0 + f2) + own
                wn[sub] = (w * (1.0 / 3.0)).astype(jnp.bfloat16)

            @pl.when(jnp.logical_not(summed))
            def _():
                w = fresh(wn[sub], f0) + own + fresh(wo[sub], f2)
                wn[sub] = (w * (1.0 / 3.0)).astype(jnp.bfloat16)

            fn[sub] = ((f0 + f1 + f2) * (1.0 / 3.0)).astype(jnp.bfloat16)
            return 0

        lax.fori_loop(0, CHUNK // PIECE, piece, 0)
        return 0

    lax.fori_loop(0, LATE, mix, 0)
    rs_x.wait_recv()
    igv[...] = ((over_y(xl) + xrecv[...].astype(jnp.float32)) * scale).astype(jnp.bfloat16)
    lax.fori_loop(LATE, chunks, mix, 0)

    def drain(n, _):
        blk = rows_of(n)
        send_near(blk, n).wait_send()
        send_out(blk, n).wait_send()
        return 0

    lax.fori_loop(0, chunks, drain, 0)
    def sent(mine, theirs):
        for cp in near_rows(theirs) + out_rows(mine) + [sums(mine)]:
            cp.wait_send()

    by_kind(sent)
    for cp in [ag_x, *ag_y0, *ag_y1, ag_c0, ag_c1, rs_c, *rs_y, rs_x, w_near, w_out]:
        cp.wait_send()


def per_device(inputs, gate_pre, grad_hidden, up_weight, momentum):
    rows, depth = inputs.shape
    tokens, width = gate_pre.shape
    chunks = depth // CHUNK
    bf = jnp.bfloat16
    any_spec = pl.BlockSpec(memory_space=pl.ANY)
    dma = pltpu.SemaphoreType.DMA
    big = pltpu.VMEM((depth, width), bf)
    ig, mw, mm = pl.pallas_call(
        kernel,
        out_shape=(pltpu.VMEM((rows, depth), bf), big, big),
        in_specs=[any_spec] * 5,
        out_specs=(pl.BlockSpec(memory_space=pltpu.VMEM),) * 3,
        scratch_shapes=[
            big,
            big,
            pltpu.VMEM((tokens, width), bf),
            pltpu.VMEM((2, 4, 2, rows, depth), bf),
            pltpu.VMEM((8, 2, rows, depth), bf),
            pltpu.VMEM((8, rows, depth), bf),
            pltpu.VMEM((3, 2, rows, depth), bf),
            pltpu.VMEM((rows, depth), bf),
            pltpu.VMEM((rows, depth), bf),
            big,
            big,
            pltpu.VMEM((max(sum(INNER_ROWS), sum(OUTER_ROWS)), width), bf),
            dma((5,)),
            dma((2, 3)),
            dma((2, 3)),
            dma((9,)),
            dma((9,)),
            dma((8,)),
            dma((8,)),
            dma((2, chunks)),
            dma((2, chunks)),
            dma((3,)),
            dma((3,)),
            pltpu.SemaphoreType.REGULAR((2,)),
        ],
        compiler_params=pltpu.CompilerParams(
            collective_id=0, has_side_effects=True, vmem_limit_bytes=50 * 2**20
        ),
        name="step",
    )(inputs, gate_pre, grad_hidden, up_weight[0], momentum[0])
    return ig, mw[None], mm[None]


def solution(mesh):
    in_specs = (
        P(("rep", "tp"), None),
        P("rep", "tp"),
        P("rep", "tp"),
        P("rep", None, "tp"),
        P("rep", None, "tp"),
    )
    out_specs = (P(("rep", "tp"), None), P("rep", None, "tp"), P("rep", None, "tp"))
    return jax.shard_map(
        per_device, mesh=mesh, in_specs=in_specs, out_specs=out_specs, check_vma=False
    )
```

```python
import jax
import jax.numpy as jnp
from jax import lax
from jax.experimental import pallas as pl
from jax.experimental.pallas import tpu as pltpu
from jax.sharding import PartitionSpec as P

momentum_beta = 0.9
learn_rate = 0.1
CHUNK = 256
SEND = 128
INNER_ROWS = (608,)
OUTER_ROWS = (256, 256)
PIECE = 32
FIRST = 8
LATE = 14
BURST = 2
MESH = pl.DeviceIdType.MESH


def kernel(
    x_hbm, a_hbm, h_hbm, w_hbm, m_hbm,
    igv, wn, fn,
    wv, fv, g, xall, part, crecv, yrecv, tup, tdown, xsend, xrecv, wo, fo,
    relw,
    loc, wsem_s, wsem_r, ag_s, ag_r, rs_s, rs_r, f_s, f_r, rel_s, rel_r, grants,
):
    depth, width = wv.shape
    rows = x_hbm.shape[0]
    tokens = g.shape[0]
    chunks = depth // CHUNK
    sends = depth // SEND
    scale = depth ** (-0.5)
    rep = lax.axis_index("rep")
    tp = lax.axis_index("tp")
    c = lax.rem(tp, 2)
    y = lax.rem(lax.div(tp, 2), 4)
    xl = lax.div(tp, 8)
    yu, yd = lax.rem(y + 1, 4), lax.rem(y + 3, 4)
    yup, ydown = [(rep, xl * 8 + yk * 2 + c) for yk in (yu, yd)]
    half = rows // 2
    lower, upper = pl.ds(0, half), pl.ds(half, half)
    odd = lax.rem(rep, 2)
    quad = lax.rem(rep, 4)
    inner = jnp.logical_or(quad == 1, quad == 2)
    near = (rep + 1 - 2 * odd, tp)
    out = (lax.rem(rep + 7 + 2 * odd, 8), tp)
    across = (jnp.where(inner, 7 - rep, 3 - rep + 8 * lax.div(rep, 4)), tp)
    xother = (rep, tp + 8 - 16 * xl)
    cother = (rep, tp + 1 - 2 * c)
    outs = (out, (out[0], cother[1]))
    inner_rows, outer_rows, at = [], [], 0
    for sizes, blocks in ((INNER_ROWS, inner_rows), (OUTER_ROWS, outer_rows)):
        for size in sizes:
            blocks.append(pl.ds(at, size))
            at += size
    rest = pl.ds(at, depth - at)

    def by_kind(run):
        pl.when(inner)(lambda: run(inner_rows, outer_rows))
        pl.when(jnp.logical_not(inner))(lambda: run(outer_rows, inner_rows))

    def remote(src, dst, s, r, dev):
        return pltpu.make_async_remote_copy(
            src_ref=src, dst_ref=dst, send_sem=s, recv_sem=r, device_id=dev, device_id_type=MESH
        )

    load_a = pltpu.make_async_copy(a_hbm, fv.at[pl.ds(0, tokens)], loc.at[0])
    load_h = pltpu.make_async_copy(h_hbm, g, loc.at[1])
    load_w = pltpu.make_async_copy(w_hbm, wv, loc.at[2])
    load_x = pltpu.make_async_copy(x_hbm, xall.at[xl, y, c], loc.at[3])
    load_m = pltpu.make_async_copy(m_hbm, fv, loc.at[4])
    load_a.start()
    load_h.start()
    load_w.start()
    load_x.start()

    barrier = pltpu.get_barrier_semaphore()
    for dev in [near, *outs, across, xother, cother, yup, ydown]:
        pl.semaphore_signal(barrier, inc=1, device_id=dev, device_id_type=MESH)
    pl.semaphore_wait(barrier, 8)

    own = xall.at[xl, y, c]
    ag_x = remote(x_hbm, own, ag_s.at[0], ag_r.at[0], xother)
    ag_y0 = [
        remote(x_hbm, own, ag_s.at[1], ag_r.at[1], yup),
        remote(x_hbm, own, ag_s.at[2], ag_r.at[2], ydown),
    ]

    def passed(u, i):
        from_down, from_up = xall.at[u, yd, c, lower], xall.at[u, yu, c, upper]
        return [
            remote(from_down, from_down, ag_s.at[i], ag_r.at[i], yup),
            remote(from_up, from_up, ag_s.at[i + 1], ag_r.at[i + 1], ydown),
        ]

    ag_y0p = passed(xl, 3)
    ag_y1p = passed(1 - xl, 7)
    w_near = remote(w_hbm.at[rest], wn.at[rest], wsem_s.at[0, 2], wsem_r.at[0, 2], near)
    w_out = remote(w_hbm.at[rest], wo.at[rest], wsem_s.at[1, 2], wsem_r.at[1, 2], out)

    def near_rows(blocks):
        return [
            remote(w_hbm.at[blk], wn.at[blk], wsem_s.at[0, i], wsem_r.at[0, i], near)
            for i, blk in enumerate(blocks)
        ]

    def out_rows(blocks):
        return [
            remote(w_hbm.at[blk], wo.at[blk], wsem_s.at[1, i], wsem_r.at[1, i], out)
            for i, blk in enumerate(blocks)
        ]

    def relays(blocks):
        return [
            remote(
                wn.at[blk],
                relw.at[pl.ds(blk.start - blocks[0].start, blk.size)],
                rel_s.at[i],
                rel_r.at[i],
                across,
            )
            for i, blk in enumerate(blocks)
        ]

    def sums(blocks):
        size = sum(blk.size for blk in blocks)
        return remote(
            relw.at[pl.ds(0, size)],
            wn.at[pl.ds(blocks[0].start, size)],
            rel_s.at[2],
            rel_r.at[2],
            near,
        )

    def pass_on(blocks, i):
        near_rows(blocks)[i].wait_recv()
        relays(blocks)[i].start()

    def granted(i):
        relays(outer_rows)[i].wait_recv()
        for dev in outs:
            pl.semaphore_signal(grants.at[i], inc=1, device_id=dev, device_id_type=MESH)
        pl.semaphore_wait(grants.at[i], 2)

    for cp in ag_y0:
        cp.start()

    @pl.when(inner)
    def _():
        ag_x.start()
        for cp in near_rows(outer_rows) + out_rows(inner_rows) + [w_near, w_out]:
            cp.start()

    @pl.when(jnp.logical_not(inner))
    def _():
        out_rows(outer_rows)[0].start()
        ag_x.start()
        for cp in near_rows(inner_rows) + [w_near]:
            cp.start()

    load_a.wait()
    load_h.wait()

    def act(i, _):
        blk = pl.ds(i * 64, 64)
        v = fv[blk].astype(jnp.float32)
        g[blk] = (g[blk].astype(jnp.float32) * (v / (1.0 + jnp.exp(-v)))).astype(jnp.bfloat16)
        return 0

    lax.fori_loop(0, tokens // 64, act, 0)
    load_m.start()

    pl.when(jnp.logical_not(inner))(lambda: pass_on(outer_rows, 0))

    for cp in ag_y0:
        cp.wait_recv()
    for cp in ag_y0p:
        cp.start()

    load_w.wait()

    def cot(n, _):
        cols = pl.ds(pl.multiple_of(n * CHUNK, CHUNK), CHUNK)
        res = lax.dot_general(
            g[...], wv[cols], (((1,), (1,)), ((), ())), preferred_element_type=jnp.float32
        )
        part[:, :, :, :, cols] = res.astype(jnp.bfloat16).reshape(2, 4, 2, rows, CHUNK)
        return 0

    lax.fori_loop(0, chunks, cot, 0)
    rs_c = remote(part.at[:, :, 1 - c], crecv, rs_s.at[0], rs_r.at[0], cother)
    rs_c.start()

    far = xall.at[1 - xl, y, c]
    ag_x.wait_recv()
    ag_y1 = [
        remote(far, far, ag_s.at[5], ag_r.at[5], yup),
        remote(far, far, ag_s.at[6], ag_r.at[6], ydown),
    ]
    for cp in ag_y1:
        cp.start()

    pl.when(inner)(lambda: pass_on(inner_rows, 0))

    @pl.when(jnp.logical_not(inner))
    def _():
        relays(outer_rows)[0].wait_send()
        out_rows(outer_rows)[1].start()
        pass_on(outer_rows, 1)
        granted(0)
        w_out.start()

    load_x.wait()
    for cp in ag_y0p:
        cp.wait_recv()
    ag_c0 = remote(xall.at[xl, :, c], xall.at[xl, :, c], ag_s.at[9], ag_r.at[9], cother)
    ag_c0.start()
    for cp in ag_y1:
        cp.wait_recv()
    for cp in ag_y1p:
        cp.start()

    rs_c.wait_recv()

    def add_core(b, _):
        u, v = lax.div(b, 4), lax.rem(b, 4)
        total = part[u, v, c].astype(jnp.float32) + crecv[u, v].astype(jnp.float32)
        crecv[u, v] = total.astype(jnp.bfloat16)
        return 0

    lax.fori_loop(0, 8, add_core, 0)

    far_y = lax.rem(y + 2, 4)

    def scatter(src, dst, i, dev):
        return remote(src, dst, rs_s.at[i], rs_r.at[i], dev)

    transit = [
        scatter(crecv.at[:, far_y, lower], tup, 1, yup),
        scatter(crecv.at[:, far_y, upper], tdown, 2, ydown),
    ]
    ready = [
        scatter(crecv.at[:, yu, upper], yrecv.at[0, :, upper], 3, yup),
        scatter(crecv.at[:, yd, lower], yrecv.at[1, :, lower], 4, ydown),
    ]
    joined = [
        scatter(crecv.at[:, yu, lower], yrecv.at[0, :, lower], 5, yup),
        scatter(crecv.at[:, yd, upper], yrecv.at[1, :, upper], 6, ydown),
    ]
    for cp in transit + ready:
        cp.start()

    for cp in ag_y1p:
        cp.wait_recv()
    ag_c1 = remote(xall.at[1 - xl, :, c], xall.at[1 - xl, :, c], ag_s.at[10], ag_r.at[10], cother)
    ag_c1.start()
    ag_c0.wait_recv()
    ag_c1.wait_recv()
    load_m.wait()

    def send_near(blk, n):
        return remote(fv.at[blk], fn.at[blk], f_s.at[0, n], f_r.at[0, n], near)

    def send_out(blk, n):
        return remote(fv.at[blk], fo.at[blk], f_s.at[1, n], f_r.at[1, n], out)

    def moment(blk):
        xs = xall[:, :, :, :, blk].reshape(tokens, CHUNK)
        delta = lax.dot_general(
            xs, g[...], (((0,), (0,)), ((), ())), preferred_element_type=jnp.float32
        )
        fv[blk] = (momentum_beta * fv[blk].astype(jnp.float32) + delta * scale).astype(jnp.bfloat16)

    def rows_of(n, size=SEND):
        return pl.ds(pl.multiple_of(n * size, size), size)

    def moments(n, _):
        moment(rows_of(n, CHUNK))
        return 0

    def send(lo, hi, *ways):
        def go(n, _):
            for way in ways:
                way(rows_of(n), n).start()
            return 0

        lax.fori_loop(lo, hi, go, 0)

    def early(n, _):
        moments(n, 0)
        for i in range(CHUNK // SEND):
            block = n * (CHUNK // SEND) + i
            send_near(rows_of(block), block).start()
            pl.when(inner)(lambda: send_out(rows_of(block), block).start())
        return 0

    lax.fori_loop(0, FIRST * SEND // CHUNK, early, 0)

    for cp in transit:
        cp.wait_recv()
    for u in range(2):
        crecv[u, yu, lower] = (
            crecv[u, yu, lower].astype(jnp.float32) + tup[u].astype(jnp.float32)
        ).astype(jnp.bfloat16)
        crecv[u, yd, upper] = (
            crecv[u, yd, upper].astype(jnp.float32) + tdown[u].astype(jnp.float32)
        ).astype(jnp.bfloat16)
    for cp in joined:
        cp.start()

    lax.fori_loop(FIRST * SEND // CHUNK, chunks, moments, 0)

    def send_sum(mine):
        size = sum(blk.size for blk in mine)

        def add_own(i, _):
            here = pl.ds(pl.multiple_of(i * PIECE, PIECE), PIECE)
            sub = pl.ds(pl.multiple_of(mine[0].start + i * PIECE, PIECE), PIECE)
            relw[here] = (relw[here].astype(jnp.float32) + wv[sub].astype(jnp.float32)).astype(jnp.bfloat16)
            return 0

        lax.fori_loop(0, size // PIECE, add_own, 0)
        sums(mine).start()

    @pl.when(inner)
    def _():
        relays(inner_rows)[0].wait_recv()
        send_sum(inner_rows)

    for cp in ready + joined:
        cp.wait_recv()

    def over_y(u):
        return (
            crecv[u, y].astype(jnp.float32)
            + yrecv[0, u].astype(jnp.float32)
            + yrecv[1, u].astype(jnp.float32)
        )

    xsend[...] = over_y(1 - xl).astype(jnp.bfloat16)
    rs_x = remote(xsend, xrecv, rs_s.at[7], rs_r.at[7], xother)
    pl.when(jnp.logical_not(inner))(lambda: w_out.wait_send())
    rs_x.start()
    pl.when(inner)(lambda: send(FIRST, sends, send_near, send_out))

    @pl.when(jnp.logical_not(inner))
    def _():
        relays(outer_rows)[1].wait_send()
        send(0, BURST, send_out)
        granted(1)
        send(BURST, sends, send_out)
        send_sum(outer_rows)
        send(FIRST, sends, send_near)

    w_near.wait_recv()
    w_out.wait_recv()

    def last_rows(mine, theirs):
        for cp in out_rows(mine):
            cp.wait_recv()
        sums(theirs).wait_recv()

    by_kind(last_rows)

    @pl.when(inner)
    def _():
        relays(inner_rows)[0].wait_send()
        w_out.wait_send()

    low = jnp.where(inner, outer_rows[0].start, 0)
    high = jnp.where(inner, rest.start, outer_rows[0].start)

    def fresh(w, f):
        return (w.astype(jnp.float32) - learn_rate * f).astype(jnp.bfloat16).astype(jnp.float32)

    def mix(n, _):
        blk = rows_of(n)
        send_near(blk, n).wait_recv()
        send_out(blk, n).wait_recv()

        def piece(i, _):
            start = n * SEND + i * PIECE
            sub = pl.ds(pl.multiple_of(start, PIECE), PIECE)
            summed = jnp.logical_and(start >= low, start < high)
            f0, f1, f2 = (r[sub].astype(jnp.float32) for r in (fn, fv, fo))
            own = fresh(wv[sub], f1)

            @pl.when(summed)
            def _():
                w = wn[sub].astype(jnp.float32) - learn_rate * (f0 + f2) + own
                wn[sub] = (w * (1.0 / 3.0)).astype(jnp.bfloat16)

            @pl.when(jnp.logical_not(summed))
            def _():
                w = fresh(wn[sub], f0) + own + fresh(wo[sub], f2)
                wn[sub] = (w * (1.0 / 3.0)).astype(jnp.bfloat16)

            fn[sub] = ((f0 + f1 + f2) * (1.0 / 3.0)).astype(jnp.bfloat16)
            return 0

        lax.fori_loop(0, SEND // PIECE, piece, 0)
        return 0

    lax.fori_loop(0, LATE, mix, 0)
    rs_x.wait_recv()
    igv[...] = ((over_y(xl) + xrecv[...].astype(jnp.float32)) * scale).astype(jnp.bfloat16)
    lax.fori_loop(LATE, sends, mix, 0)

    def drain(n, _):
        blk = rows_of(n)
        send_near(blk, n).wait_send()
        send_out(blk, n).wait_send()
        return 0

    lax.fori_loop(0, sends, drain, 0)
    def sent(mine, theirs):
        for cp in near_rows(theirs) + out_rows(mine) + [sums(mine)]:
            cp.wait_send()

    by_kind(sent)
    gathers = [ag_x, *ag_y0, *ag_y0p, *ag_y1, *ag_y1p, ag_c0, ag_c1]
    for cp in gathers + [rs_c, *transit, *ready, *joined, rs_x, w_near]:
        cp.wait_send()


def per_device(inputs, gate_pre, grad_hidden, up_weight, momentum):
    rows, depth = inputs.shape
    tokens, width = gate_pre.shape
    sends = depth // SEND
    bf = jnp.bfloat16
    any_spec = pl.BlockSpec(memory_space=pl.ANY)
    dma = pltpu.SemaphoreType.DMA
    big = pltpu.VMEM((depth, width), bf)
    ig, mw, mm = pl.pallas_call(
        kernel,
        out_shape=(pltpu.VMEM((rows, depth), bf), big, big),
        in_specs=[any_spec] * 5,
        out_specs=(pl.BlockSpec(memory_space=pltpu.VMEM),) * 3,
        scratch_shapes=[
            big,
            big,
            pltpu.VMEM((tokens, width), bf),
            pltpu.VMEM((2, 4, 2, rows, depth), bf),
            pltpu.VMEM((2, 4, 2, rows, depth), bf),
            pltpu.VMEM((2, 4, rows, depth), bf),
            pltpu.VMEM((2, 2, rows, depth), bf),
            pltpu.VMEM((2, rows // 2, depth), bf),
            pltpu.VMEM((2, rows // 2, depth), bf),
            pltpu.VMEM((rows, depth), bf),
            pltpu.VMEM((rows, depth), bf),
            big,
            big,
            pltpu.VMEM((max(sum(INNER_ROWS), sum(OUTER_ROWS)), width), bf),
            dma((5,)),
            dma((2, 3)),
            dma((2, 3)),
            dma((11,)),
            dma((11,)),
            dma((8,)),
            dma((8,)),
            dma((2, sends)),
            dma((2, sends)),
            dma((3,)),
            dma((3,)),
            pltpu.SemaphoreType.REGULAR((2,)),
        ],
        compiler_params=pltpu.CompilerParams(
            collective_id=0, has_side_effects=True, vmem_limit_bytes=50 * 2**20
        ),
        name="step",
    )(inputs, gate_pre, grad_hidden, up_weight[0], momentum[0])
    return ig, mw[None], mm[None]


def solution(mesh):
    in_specs = (
        P(("rep", "tp"), None),
        P("rep", "tp"),
        P("rep", "tp"),
        P("rep", None, "tp"),
        P("rep", None, "tp"),
    )
    out_specs = (P(("rep", "tp"), None), P("rep", None, "tp"), P("rep", None, "tp"))
    return jax.shard_map(
        per_device, mesh=mesh, in_specs=in_specs, out_specs=out_specs, check_vma=False
    )
```

```python
import jax
import jax.numpy as jnp
from jax import lax
from jax.experimental import pallas as pl
from jax.experimental.pallas import tpu as pltpu
from jax.sharding import PartitionSpec as P

momentum_beta = 0.9
learn_rate = 0.1
CHUNK = 256
SEND = 128
INNER_ROWS = (608,)
OUTER_ROWS = (256, 256)
PIECE = 32
FIRST = 8
LATE = 14
STORES = 4
BURST = 2
MESH = pl.DeviceIdType.MESH


def kernel(
    x_hbm, a_hbm, h_hbm, w_hbm, m_hbm,
    igv, wn, fn,
    wv, fv, g, xall, part, crecv, yrecv, tup, tdown, xsend, xrecv, wo, fo,
    relw,
    loc, wsem_s, wsem_r, ag_s, ag_r, rs_s, rs_r, f_s, f_r, rel_s, rel_r, grants,
):
    depth, width = wv.shape
    rows = x_hbm.shape[0]
    tokens = g.shape[0]
    chunks = depth // CHUNK
    sends = depth // SEND
    scale = depth ** (-0.5)
    rep = lax.axis_index("rep")
    tp = lax.axis_index("tp")
    c = lax.rem(tp, 2)
    y = lax.rem(lax.div(tp, 2), 4)
    xl = lax.div(tp, 8)
    yu, yd = lax.rem(y + 1, 4), lax.rem(y + 3, 4)
    yup, ydown = [(rep, xl * 8 + yk * 2 + c) for yk in (yu, yd)]
    half = rows // 2
    lower, upper = pl.ds(0, half), pl.ds(half, half)
    odd = lax.rem(rep, 2)
    quad = lax.rem(rep, 4)
    inner = jnp.logical_or(quad == 1, quad == 2)
    near = (rep + 1 - 2 * odd, tp)
    out = (lax.rem(rep + 7 + 2 * odd, 8), tp)
    across = (jnp.where(inner, 7 - rep, 3 - rep + 8 * lax.div(rep, 4)), tp)
    xother = (rep, tp + 8 - 16 * xl)
    cother = (rep, tp + 1 - 2 * c)
    outs = (out, (out[0], cother[1]))
    inner_rows, outer_rows, at = [], [], 0
    for sizes, blocks in ((INNER_ROWS, inner_rows), (OUTER_ROWS, outer_rows)):
        for size in sizes:
            blocks.append(pl.ds(at, size))
            at += size
    rest = pl.ds(at, depth - at)

    def by_kind(run):
        pl.when(inner)(lambda: run(inner_rows, outer_rows))
        pl.when(jnp.logical_not(inner))(lambda: run(outer_rows, inner_rows))

    def remote(src, dst, s, r, dev):
        return pltpu.make_async_remote_copy(
            src_ref=src, dst_ref=dst, send_sem=s, recv_sem=r, device_id=dev, device_id_type=MESH
        )

    load_a = pltpu.make_async_copy(a_hbm, fv.at[pl.ds(0, tokens)], loc.at[0])
    load_h = pltpu.make_async_copy(h_hbm, g, loc.at[1])
    load_w = pltpu.make_async_copy(w_hbm, wv, loc.at[2])
    load_x = pltpu.make_async_copy(x_hbm, xall.at[xl, y, c], loc.at[3])
    load_m = pltpu.make_async_copy(m_hbm, fv, loc.at[4])
    load_a.start()
    load_h.start()
    load_w.start()
    load_x.start()

    barrier = pltpu.get_barrier_semaphore()
    for dev in [near, *outs, across, xother, cother, yup, ydown]:
        pl.semaphore_signal(barrier, inc=1, device_id=dev, device_id_type=MESH)
    pl.semaphore_wait(barrier, 8)

    own = xall.at[xl, y, c]
    ag_x = remote(x_hbm, own, ag_s.at[0], ag_r.at[0], xother)
    ag_y0 = [
        remote(x_hbm, own, ag_s.at[1], ag_r.at[1], yup),
        remote(x_hbm, own, ag_s.at[2], ag_r.at[2], ydown),
    ]

    def passed(u, i):
        from_down, from_up = xall.at[u, yd, c, lower], xall.at[u, yu, c, upper]
        return [
            remote(from_down, from_down, ag_s.at[i], ag_r.at[i], yup),
            remote(from_up, from_up, ag_s.at[i + 1], ag_r.at[i + 1], ydown),
        ]

    ag_y0p = passed(xl, 3)
    ag_y1p = passed(1 - xl, 7)
    w_near = remote(w_hbm.at[rest], wn.at[rest], wsem_s.at[0, 2], wsem_r.at[0, 2], near)
    w_out = remote(w_hbm.at[rest], wo.at[rest], wsem_s.at[1, 2], wsem_r.at[1, 2], out)

    def near_rows(blocks):
        return [
            remote(w_hbm.at[blk], wn.at[blk], wsem_s.at[0, i], wsem_r.at[0, i], near)
            for i, blk in enumerate(blocks)
        ]

    def out_rows(blocks):
        return [
            remote(w_hbm.at[blk], wo.at[blk], wsem_s.at[1, i], wsem_r.at[1, i], out)
            for i, blk in enumerate(blocks)
        ]

    def relays(blocks):
        return [
            remote(
                wn.at[blk],
                relw.at[pl.ds(blk.start - blocks[0].start, blk.size)],
                rel_s.at[i],
                rel_r.at[i],
                across,
            )
            for i, blk in enumerate(blocks)
        ]

    def sums(blocks):
        size = sum(blk.size for blk in blocks)
        return remote(
            relw.at[pl.ds(0, size)],
            wn.at[pl.ds(blocks[0].start, size)],
            rel_s.at[2],
            rel_r.at[2],
            near,
        )

    def pass_on(blocks, i):
        near_rows(blocks)[i].wait_recv()
        relays(blocks)[i].start()

    def granted(i):
        relays(outer_rows)[i].wait_recv()
        for dev in outs:
            pl.semaphore_signal(grants.at[i], inc=1, device_id=dev, device_id_type=MESH)
        pl.semaphore_wait(grants.at[i], 2)

    for cp in ag_y0:
        cp.start()

    @pl.when(inner)
    def _():
        ag_x.start()
        for cp in near_rows(outer_rows) + out_rows(inner_rows) + [w_near, w_out]:
            cp.start()

    @pl.when(jnp.logical_not(inner))
    def _():
        out_rows(outer_rows)[0].start()
        ag_x.start()
        for cp in near_rows(inner_rows) + [w_near]:
            cp.start()

    load_a.wait()
    load_h.wait()

    def act(i, _):
        blk = pl.ds(i * 64, 64)
        v = fv[blk].astype(jnp.float32)
        g[blk] = (g[blk].astype(jnp.float32) * (v / (1.0 + jnp.exp(-v)))).astype(jnp.bfloat16)
        return 0

    lax.fori_loop(0, tokens // 64, act, 0)
    load_m.start()

    pl.when(jnp.logical_not(inner))(lambda: pass_on(outer_rows, 0))

    for cp in ag_y0:
        cp.wait_recv()
    for cp in ag_y0p:
        cp.start()

    load_w.wait()

    def cot(n, _):
        cols = pl.ds(pl.multiple_of(n * CHUNK, CHUNK), CHUNK)
        res = lax.dot_general(
            g[...], wv[cols], (((1,), (1,)), ((), ())), preferred_element_type=jnp.float32
        )
        part[:, :, :, :, cols] = res.astype(jnp.bfloat16).reshape(2, 4, 2, rows, CHUNK)
        return 0

    lax.fori_loop(0, chunks, cot, 0)
    rs_c = remote(part.at[:, :, 1 - c], crecv, rs_s.at[0], rs_r.at[0], cother)
    rs_c.start()

    far = xall.at[1 - xl, y, c]
    ag_x.wait_recv()
    ag_y1 = [
        remote(far, far, ag_s.at[5], ag_r.at[5], yup),
        remote(far, far, ag_s.at[6], ag_r.at[6], ydown),
    ]
    for cp in ag_y1:
        cp.start()

    pl.when(inner)(lambda: pass_on(inner_rows, 0))

    @pl.when(jnp.logical_not(inner))
    def _():
        relays(outer_rows)[0].wait_send()
        out_rows(outer_rows)[1].start()
        pass_on(outer_rows, 1)
        granted(0)
        w_out.start()

    load_x.wait()
    for cp in ag_y0p:
        cp.wait_recv()
    ag_c0 = remote(xall.at[xl, :, c], xall.at[xl, :, c], ag_s.at[9], ag_r.at[9], cother)
    ag_c0.start()
    for cp in ag_y1:
        cp.wait_recv()
    for cp in ag_y1p:
        cp.start()

    rs_c.wait_recv()

    def add_core(b, _):
        u, v = lax.div(b, 4), lax.rem(b, 4)
        total = part[u, v, c].astype(jnp.float32) + crecv[u, v].astype(jnp.float32)
        crecv[u, v] = total.astype(jnp.bfloat16)
        return 0

    lax.fori_loop(0, 8, add_core, 0)

    far_y = lax.rem(y + 2, 4)

    def scatter(src, dst, i, dev):
        return remote(src, dst, rs_s.at[i], rs_r.at[i], dev)

    transit = [
        scatter(crecv.at[:, far_y, lower], tup, 1, yup),
        scatter(crecv.at[:, far_y, upper], tdown, 2, ydown),
    ]
    ready = [
        scatter(crecv.at[:, yu, upper], yrecv.at[0, :, upper], 3, yup),
        scatter(crecv.at[:, yd, lower], yrecv.at[1, :, lower], 4, ydown),
    ]
    joined = [
        scatter(crecv.at[:, yu, lower], yrecv.at[0, :, lower], 5, yup),
        scatter(crecv.at[:, yd, upper], yrecv.at[1, :, upper], 6, ydown),
    ]
    for cp in transit + ready:
        cp.start()

    for cp in ag_y1p:
        cp.wait_recv()
    ag_c1 = remote(xall.at[1 - xl, :, c], xall.at[1 - xl, :, c], ag_s.at[10], ag_r.at[10], cother)
    ag_c1.start()
    ag_c0.wait_recv()
    ag_c1.wait_recv()
    load_m.wait()

    def send_near(blk, n):
        return remote(fv.at[blk], fn.at[blk], f_s.at[0, n], f_r.at[0, n], near)

    def send_out(blk, n):
        return remote(fv.at[blk], fo.at[blk], f_s.at[1, n], f_r.at[1, n], out)

    def moment(blk):
        xs = xall[:, :, :, :, blk].reshape(tokens, CHUNK)
        delta = lax.dot_general(
            xs, g[...], (((0,), (0,)), ((), ())), preferred_element_type=jnp.float32
        )
        fv[blk] = (momentum_beta * fv[blk].astype(jnp.float32) + delta * scale).astype(jnp.bfloat16)

    def rows_of(n, size=SEND):
        return pl.ds(pl.multiple_of(n * size, size), size)

    def moments(n, _):
        moment(rows_of(n, CHUNK))
        return 0

    def send(lo, hi, *ways):
        def go(n, _):
            for way in ways:
                way(rows_of(n), n).start()
            return 0

        lax.fori_loop(lo, hi, go, 0)

    def early(n, _):
        moments(n, 0)
        for i in range(CHUNK // SEND):
            block = n * (CHUNK // SEND) + i
            send_near(rows_of(block), block).start()
            pl.when(inner)(lambda: send_out(rows_of(block), block).start())
        return 0

    lax.fori_loop(0, FIRST * SEND // CHUNK, early, 0)

    for cp in transit:
        cp.wait_recv()
    for u in range(2):
        crecv[u, yu, lower] = (
            crecv[u, yu, lower].astype(jnp.float32) + tup[u].astype(jnp.float32)
        ).astype(jnp.bfloat16)
        crecv[u, yd, upper] = (
            crecv[u, yd, upper].astype(jnp.float32) + tdown[u].astype(jnp.float32)
        ).astype(jnp.bfloat16)
    for cp in joined:
        cp.start()

    lax.fori_loop(FIRST * SEND // CHUNK, chunks, moments, 0)

    def send_sum(mine):
        size = sum(blk.size for blk in mine)

        def add_own(i, _):
            here = pl.ds(pl.multiple_of(i * PIECE, PIECE), PIECE)
            sub = pl.ds(pl.multiple_of(mine[0].start + i * PIECE, PIECE), PIECE)
            relw[here] = (relw[here].astype(jnp.float32) + wv[sub].astype(jnp.float32)).astype(jnp.bfloat16)
            return 0

        lax.fori_loop(0, size // PIECE, add_own, 0)
        sums(mine).start()

    @pl.when(inner)
    def _():
        relays(inner_rows)[0].wait_recv()
        send_sum(inner_rows)

    for cp in ready + joined:
        cp.wait_recv()

    def over_y(u):
        return (
            crecv[u, y].astype(jnp.float32)
            + yrecv[0, u].astype(jnp.float32)
            + yrecv[1, u].astype(jnp.float32)
        )

    xsend[...] = over_y(1 - xl).astype(jnp.bfloat16)
    rs_x = remote(xsend, xrecv, rs_s.at[7], rs_r.at[7], xother)
    pl.when(jnp.logical_not(inner))(lambda: w_out.wait_send())
    rs_x.start()
    pl.when(inner)(lambda: send(FIRST, sends, send_near, send_out))

    @pl.when(jnp.logical_not(inner))
    def _():
        relays(outer_rows)[1].wait_send()
        send(0, BURST, send_out)
        granted(1)
        send(BURST, sends, send_out)
        send_sum(outer_rows)
        send(FIRST, sends, send_near)

    w_near.wait_recv()
    w_out.wait_recv()

    def last_rows(mine, theirs):
        for cp in out_rows(mine):
            cp.wait_recv()
        sums(theirs).wait_recv()

    by_kind(last_rows)

    @pl.when(inner)
    def _():
        relays(inner_rows)[0].wait_send()
        w_out.wait_send()

    low = jnp.where(inner, outer_rows[0].start, 0)
    high = jnp.where(inner, rest.start, outer_rows[0].start)

    def fresh(w, f):
        return (w.astype(jnp.float32) - learn_rate * f).astype(jnp.bfloat16).astype(jnp.float32)

    def mix(n, _):
        blk = rows_of(n)
        send_near(blk, n).wait_recv()
        send_out(blk, n).wait_recv()

        def piece(i, _):
            start = n * SEND + i * PIECE
            sub = pl.ds(pl.multiple_of(start, PIECE), PIECE)
            summed = jnp.logical_and(start >= low, start < high)
            f0, f1, f2 = (r[sub].astype(jnp.float32) for r in (fn, fv, fo))
            own = fresh(wv[sub], f1)

            @pl.when(summed)
            def _():
                w = wn[sub].astype(jnp.float32) - learn_rate * (f0 + f2) + own
                wn[sub] = (w * (1.0 / 3.0)).astype(jnp.bfloat16)

            @pl.when(jnp.logical_not(summed))
            def _():
                w = fresh(wn[sub], f0) + own + fresh(wo[sub], f2)
                wn[sub] = (w * (1.0 / 3.0)).astype(jnp.bfloat16)

            fn[sub] = ((f0 + f1 + f2) * (1.0 / 3.0)).astype(jnp.bfloat16)
            return 0

        lax.fori_loop(0, SEND // PIECE, piece, 0)
        return 0

    lax.fori_loop(0, LATE, mix, 0)
    rs_x.wait_recv()
    igv[...] = ((over_y(xl) + xrecv[...].astype(jnp.float32)) * scale).astype(jnp.bfloat16)
    lax.fori_loop(LATE, sends, mix, 0)

    def drain(n, _):
        blk = rows_of(n)
        send_near(blk, n).wait_send()
        send_out(blk, n).wait_send()
        return 0

    lax.fori_loop(0, sends, drain, 0)
    def sent(mine, theirs):
        for cp in near_rows(theirs) + out_rows(mine) + [sums(mine)]:
            cp.wait_send()

    by_kind(sent)
    gathers = [ag_x, *ag_y0, *ag_y0p, *ag_y1, *ag_y1p, ag_c0, ag_c1]
    for cp in gathers + [rs_c, *transit, *ready, *joined, rs_x, w_near]:
        cp.wait_send()


def store(ig, mw, mm, ig_hbm, mw_hbm, mm_hbm, sem):
    copies = [pltpu.make_async_copy(ig, ig_hbm, sem.at[0])]
    part = mw.shape[0] // STORES
    for i in range(STORES):
        blk = pl.ds(i * part, part)
        copies.append(pltpu.make_async_copy(mw.at[blk], mw_hbm.at[blk], sem.at[1 + 2 * i]))
        copies.append(pltpu.make_async_copy(mm.at[blk], mm_hbm.at[blk], sem.at[2 + 2 * i]))
    for cp in copies:
        cp.start()
    for cp in copies:
        cp.wait()


def per_device(inputs, gate_pre, grad_hidden, up_weight, momentum):
    rows, depth = inputs.shape
    tokens, width = gate_pre.shape
    sends = depth // SEND
    bf = jnp.bfloat16
    any_spec = pl.BlockSpec(memory_space=pl.ANY)
    dma = pltpu.SemaphoreType.DMA
    big = pltpu.VMEM((depth, width), bf)
    ig, mw, mm = pl.pallas_call(
        kernel,
        out_shape=(pltpu.VMEM((rows, depth), bf), big, big),
        in_specs=[any_spec] * 5,
        out_specs=(pl.BlockSpec(memory_space=pltpu.VMEM),) * 3,
        scratch_shapes=[
            big,
            big,
            pltpu.VMEM((tokens, width), bf),
            pltpu.VMEM((2, 4, 2, rows, depth), bf),
            pltpu.VMEM((2, 4, 2, rows, depth), bf),
            pltpu.VMEM((2, 4, rows, depth), bf),
            pltpu.VMEM((2, 2, rows, depth), bf),
            pltpu.VMEM((2, rows // 2, depth), bf),
            pltpu.VMEM((2, rows // 2, depth), bf),
            pltpu.VMEM((rows, depth), bf),
            pltpu.VMEM((rows, depth), bf),
            big,
            big,
            pltpu.VMEM((max(sum(INNER_ROWS), sum(OUTER_ROWS)), width), bf),
            dma((5,)),
            dma((2, 3)),
            dma((2, 3)),
            dma((11,)),
            dma((11,)),
            dma((8,)),
            dma((8,)),
            dma((2, sends)),
            dma((2, sends)),
            dma((3,)),
            dma((3,)),
            pltpu.SemaphoreType.REGULAR((2,)),
        ],
        compiler_params=pltpu.CompilerParams(
            collective_id=0, has_side_effects=True, vmem_limit_bytes=50 * 2**20
        ),
        name="step",
    )(inputs, gate_pre, grad_hidden, up_weight[0], momentum[0])
    whole = jax.ShapeDtypeStruct((depth, width), bf)
    ig, mw, mm = pl.pallas_call(
        store,
        out_shape=(jax.ShapeDtypeStruct((rows, depth), bf), whole, whole),
        in_specs=[any_spec] * 3,
        out_specs=(any_spec,) * 3,
        scratch_shapes=[dma((1 + 2 * STORES,))],
        compiler_params=pltpu.CompilerParams(vmem_limit_bytes=2**20),
        name="store",
    )(ig, mw, mm)
    return ig, mw[None], mm[None]


def solution(mesh):
    in_specs = (
        P(("rep", "tp"), None),
        P("rep", "tp"),
        P("rep", "tp"),
        P("rep", None, "tp"),
        P("rep", None, "tp"),
    )
    out_specs = (P(("rep", "tp"), None), P("rep", None, "tp"), P("rep", None, "tp"))
    return jax.shard_map(
        per_device, mesh=mesh, in_specs=in_specs, out_specs=out_specs, check_vma=False
    )
```

```python
import jax
import jax.numpy as jnp
from jax import lax
from jax.experimental import pallas as pl
from jax.experimental.pallas import tpu as pltpu
from jax.sharding import PartitionSpec as P

momentum_beta = 0.9
learn_rate = 0.1
CHUNK = 256
SEND = 128
INNER_ROWS = (624,)
OUTER_ROWS = (256, 272)
PIECE = 16
FIRST = 8
LATE = 14
STORES = 4
BURST = 2
MESH = pl.DeviceIdType.MESH


def kernel(
    x_hbm, a_hbm, h_hbm, w_hbm, m_hbm,
    igv, wn, fn,
    wv, fv, g, xall, part, crecv, yrecv, tup, tdown, xsend, xrecv, wo, fo,
    relw,
    loc, wsem_s, wsem_r, ag_s, ag_r, rs_s, rs_r, f_s, f_r, rel_s, rel_r, grants,
):
    depth, width = wv.shape
    rows = x_hbm.shape[0]
    tokens = g.shape[0]
    chunks = depth // CHUNK
    sends = depth // SEND
    scale = depth ** (-0.5)
    rep = lax.axis_index("rep")
    tp = lax.axis_index("tp")
    c = lax.rem(tp, 2)
    y = lax.rem(lax.div(tp, 2), 4)
    xl = lax.div(tp, 8)
    yu, yd = lax.rem(y + 1, 4), lax.rem(y + 3, 4)
    yup, ydown = [(rep, xl * 8 + yk * 2 + c) for yk in (yu, yd)]
    half = rows // 2
    lower, upper = pl.ds(0, half), pl.ds(half, half)
    odd = lax.rem(rep, 2)
    quad = lax.rem(rep, 4)
    inner = jnp.logical_or(quad == 1, quad == 2)
    near = (rep + 1 - 2 * odd, tp)
    out = (lax.rem(rep + 7 + 2 * odd, 8), tp)
    across = (jnp.where(inner, 7 - rep, 3 - rep + 8 * lax.div(rep, 4)), tp)
    xother = (rep, tp + 8 - 16 * xl)
    cother = (rep, tp + 1 - 2 * c)
    outs = (out, (out[0], cother[1]))
    inner_rows, outer_rows, at = [], [], 0
    for sizes, blocks in ((INNER_ROWS, inner_rows), (OUTER_ROWS, outer_rows)):
        for size in sizes:
            blocks.append(pl.ds(at, size))
            at += size
    rest = pl.ds(at, depth - at)

    def by_kind(run):
        pl.when(inner)(lambda: run(inner_rows, outer_rows))
        pl.when(jnp.logical_not(inner))(lambda: run(outer_rows, inner_rows))

    def remote(src, dst, s, r, dev):
        return pltpu.make_async_remote_copy(
            src_ref=src, dst_ref=dst, send_sem=s, recv_sem=r, device_id=dev, device_id_type=MESH
        )

    load_a = pltpu.make_async_copy(a_hbm, fv.at[pl.ds(0, tokens)], loc.at[0])
    load_h = pltpu.make_async_copy(h_hbm, g, loc.at[1])
    load_w = pltpu.make_async_copy(w_hbm, wv, loc.at[2])
    load_x = pltpu.make_async_copy(x_hbm, xall.at[xl, y, c], loc.at[3])
    load_m = pltpu.make_async_copy(m_hbm, fv, loc.at[4])
    load_a.start()
    load_h.start()
    load_w.start()
    load_x.start()

    barrier = pltpu.get_barrier_semaphore()
    for dev in [near, *outs, across, xother, cother, yup, ydown]:
        pl.semaphore_signal(barrier, inc=1, device_id=dev, device_id_type=MESH)
    pl.semaphore_wait(barrier, 8)

    own = xall.at[xl, y, c]
    ag_x = remote(x_hbm, own, ag_s.at[0], ag_r.at[0], xother)
    ag_y0 = [
        remote(x_hbm, own, ag_s.at[1], ag_r.at[1], yup),
        remote(x_hbm, own, ag_s.at[2], ag_r.at[2], ydown),
    ]

    def passed(u, i):
        from_down, from_up = xall.at[u, yd, c, lower], xall.at[u, yu, c, upper]
        return [
            remote(from_down, from_down, ag_s.at[i], ag_r.at[i], yup),
            remote(from_up, from_up, ag_s.at[i + 1], ag_r.at[i + 1], ydown),
        ]

    ag_y0p = passed(xl, 3)
    ag_y1p = passed(1 - xl, 7)
    w_near = remote(w_hbm.at[rest], wn.at[rest], wsem_s.at[0, 2], wsem_r.at[0, 2], near)
    w_out = remote(w_hbm.at[rest], wo.at[rest], wsem_s.at[1, 2], wsem_r.at[1, 2], out)

    def near_rows(blocks):
        return [
            remote(w_hbm.at[blk], wn.at[blk], wsem_s.at[0, i], wsem_r.at[0, i], near)
            for i, blk in enumerate(blocks)
        ]

    def out_rows(blocks):
        return [
            remote(w_hbm.at[blk], wo.at[blk], wsem_s.at[1, i], wsem_r.at[1, i], out)
            for i, blk in enumerate(blocks)
        ]

    def relays(blocks):
        return [
            remote(
                wn.at[blk],
                relw.at[pl.ds(blk.start - blocks[0].start, blk.size)],
                rel_s.at[i],
                rel_r.at[i],
                across,
            )
            for i, blk in enumerate(blocks)
        ]

    def sums(blocks):
        size = sum(blk.size for blk in blocks)
        return remote(
            relw.at[pl.ds(0, size)],
            wn.at[pl.ds(blocks[0].start, size)],
            rel_s.at[2],
            rel_r.at[2],
            near,
        )

    def pass_on(blocks, i):
        near_rows(blocks)[i].wait_recv()
        relays(blocks)[i].start()

    def granted(i):
        relays(outer_rows)[i].wait_recv()
        for dev in outs:
            pl.semaphore_signal(grants.at[i], inc=1, device_id=dev, device_id_type=MESH)
        pl.semaphore_wait(grants.at[i], 2)

    for cp in ag_y0:
        cp.start()

    @pl.when(inner)
    def _():
        ag_x.start()
        for cp in near_rows(outer_rows) + out_rows(inner_rows) + [w_near, w_out]:
            cp.start()

    @pl.when(jnp.logical_not(inner))
    def _():
        out_rows(outer_rows)[0].start()
        ag_x.start()
        for cp in near_rows(inner_rows) + [w_near]:
            cp.start()

    load_a.wait()
    load_h.wait()

    def act(i, _):
        blk = pl.ds(i * 64, 64)
        v = fv[blk].astype(jnp.float32)
        g[blk] = (g[blk].astype(jnp.float32) * (v / (1.0 + jnp.exp(-v)))).astype(jnp.bfloat16)
        return 0

    lax.fori_loop(0, tokens // 64, act, 0)
    load_m.start()

    pl.when(jnp.logical_not(inner))(lambda: pass_on(outer_rows, 0))

    for cp in ag_y0:
        cp.wait_recv()
    for cp in ag_y0p:
        cp.start()

    load_w.wait()

    def cot(n, _):
        cols = pl.ds(pl.multiple_of(n * CHUNK, CHUNK), CHUNK)
        res = lax.dot_general(
            g[...], wv[cols], (((1,), (1,)), ((), ())), preferred_element_type=jnp.float32
        )
        part[:, :, :, :, cols] = res.astype(jnp.bfloat16).reshape(2, 4, 2, rows, CHUNK)
        return 0

    lax.fori_loop(0, chunks, cot, 0)
    rs_c = remote(part.at[:, :, 1 - c], crecv, rs_s.at[0], rs_r.at[0], cother)
    rs_c.start()

    far = xall.at[1 - xl, y, c]
    ag_x.wait_recv()
    ag_y1 = [
        remote(far, far, ag_s.at[5], ag_r.at[5], yup),
        remote(far, far, ag_s.at[6], ag_r.at[6], ydown),
    ]
    for cp in ag_y1:
        cp.start()

    pl.when(inner)(lambda: pass_on(inner_rows, 0))

    @pl.when(jnp.logical_not(inner))
    def _():
        relays(outer_rows)[0].wait_send()
        out_rows(outer_rows)[1].start()
        pass_on(outer_rows, 1)
        granted(0)
        w_out.start()

    load_x.wait()
    for cp in ag_y0p:
        cp.wait_recv()
    ag_c0 = remote(xall.at[xl, :, c], xall.at[xl, :, c], ag_s.at[9], ag_r.at[9], cother)
    ag_c0.start()
    for cp in ag_y1:
        cp.wait_recv()
    for cp in ag_y1p:
        cp.start()

    rs_c.wait_recv()

    def add_core(b, _):
        u, v = lax.div(b, 4), lax.rem(b, 4)
        total = part[u, v, c].astype(jnp.float32) + crecv[u, v].astype(jnp.float32)
        crecv[u, v] = total.astype(jnp.bfloat16)
        return 0

    lax.fori_loop(0, 8, add_core, 0)

    far_y = lax.rem(y + 2, 4)

    def scatter(src, dst, i, dev):
        return remote(src, dst, rs_s.at[i], rs_r.at[i], dev)

    transit = [
        scatter(crecv.at[:, far_y, lower], tup, 1, yup),
        scatter(crecv.at[:, far_y, upper], tdown, 2, ydown),
    ]
    ready = [
        scatter(crecv.at[:, yu, upper], yrecv.at[0, :, upper], 3, yup),
        scatter(crecv.at[:, yd, lower], yrecv.at[1, :, lower], 4, ydown),
    ]
    joined = [
        scatter(crecv.at[:, yu, lower], yrecv.at[0, :, lower], 5, yup),
        scatter(crecv.at[:, yd, upper], yrecv.at[1, :, upper], 6, ydown),
    ]
    for cp in transit + ready:
        cp.start()

    for cp in ag_y1p:
        cp.wait_recv()
    ag_c1 = remote(xall.at[1 - xl, :, c], xall.at[1 - xl, :, c], ag_s.at[10], ag_r.at[10], cother)
    ag_c1.start()
    ag_c0.wait_recv()
    ag_c1.wait_recv()
    load_m.wait()

    def send_near(blk, n):
        return remote(fv.at[blk], fn.at[blk], f_s.at[0, n], f_r.at[0, n], near)

    def send_out(blk, n):
        return remote(fv.at[blk], fo.at[blk], f_s.at[1, n], f_r.at[1, n], out)

    def moment(blk):
        xs = xall[:, :, :, :, blk].reshape(tokens, CHUNK)
        delta = lax.dot_general(
            xs, g[...], (((0,), (0,)), ((), ())), preferred_element_type=jnp.float32
        )
        fv[blk] = (momentum_beta * fv[blk].astype(jnp.float32) + delta * scale).astype(jnp.bfloat16)

    def rows_of(n, size=SEND):
        return pl.ds(pl.multiple_of(n * size, size), size)

    def moments(n, _):
        moment(rows_of(n, CHUNK))
        return 0

    def send(lo, hi, *ways):
        def go(n, _):
            for way in ways:
                way(rows_of(n), n).start()
            return 0

        lax.fori_loop(lo, hi, go, 0)

    def early(n, _):
        moments(n, 0)
        for i in range(CHUNK // SEND):
            block = n * (CHUNK // SEND) + i
            send_near(rows_of(block), block).start()
            pl.when(inner)(lambda: send_out(rows_of(block), block).start())
        return 0

    lax.fori_loop(0, FIRST * SEND // CHUNK, early, 0)

    for cp in transit:
        cp.wait_recv()
    for u in range(2):
        crecv[u, yu, lower] = (
            crecv[u, yu, lower].astype(jnp.float32) + tup[u].astype(jnp.float32)
        ).astype(jnp.bfloat16)
        crecv[u, yd, upper] = (
            crecv[u, yd, upper].astype(jnp.float32) + tdown[u].astype(jnp.float32)
        ).astype(jnp.bfloat16)
    for cp in joined:
        cp.start()

    lax.fori_loop(FIRST * SEND // CHUNK, chunks, moments, 0)

    def send_sum(mine):
        size = sum(blk.size for blk in mine)

        def add_own(i, _):
            here = pl.ds(pl.multiple_of(i * PIECE, PIECE), PIECE)
            sub = pl.ds(pl.multiple_of(mine[0].start + i * PIECE, PIECE), PIECE)
            relw[here] = (relw[here].astype(jnp.float32) + wv[sub].astype(jnp.float32)).astype(jnp.bfloat16)
            return 0

        lax.fori_loop(0, size // PIECE, add_own, 0)
        sums(mine).start()

    @pl.when(inner)
    def _():
        relays(inner_rows)[0].wait_recv()
        send_sum(inner_rows)

    for cp in ready + joined:
        cp.wait_recv()

    def over_y(u):
        return (
            crecv[u, y].astype(jnp.float32)
            + yrecv[0, u].astype(jnp.float32)
            + yrecv[1, u].astype(jnp.float32)
        )

    xsend[...] = over_y(1 - xl).astype(jnp.bfloat16)
    rs_x = remote(xsend, xrecv, rs_s.at[7], rs_r.at[7], xother)
    pl.when(jnp.logical_not(inner))(lambda: w_out.wait_send())
    rs_x.start()
    pl.when(inner)(lambda: send(FIRST, sends, send_near, send_out))

    @pl.when(jnp.logical_not(inner))
    def _():
        relays(outer_rows)[1].wait_send()
        send(0, BURST, send_out)
        granted(1)
        send(BURST, sends, send_out)
        send_sum(outer_rows)
        send(FIRST, sends, send_near)

    w_near.wait_recv()
    w_out.wait_recv()

    def last_rows(mine, theirs):
        for cp in out_rows(mine):
            cp.wait_recv()
        sums(theirs).wait_recv()

    by_kind(last_rows)

    @pl.when(inner)
    def _():
        relays(inner_rows)[0].wait_send()
        w_out.wait_send()

    low = jnp.where(inner, outer_rows[0].start, 0)
    high = jnp.where(inner, rest.start, outer_rows[0].start)

    def fresh(w, f):
        return (w.astype(jnp.float32) - learn_rate * f).astype(jnp.bfloat16).astype(jnp.float32)

    def mix(n, _):
        blk = rows_of(n)
        send_near(blk, n).wait_recv()
        send_out(blk, n).wait_recv()

        def piece(i, _):
            start = n * SEND + i * PIECE
            sub = pl.ds(pl.multiple_of(start, PIECE), PIECE)
            summed = jnp.logical_and(start >= low, start < high)
            f0, f1, f2 = (r[sub].astype(jnp.float32) for r in (fn, fv, fo))
            own = fresh(wv[sub], f1)

            @pl.when(summed)
            def _():
                w = wn[sub].astype(jnp.float32) - learn_rate * (f0 + f2) + own
                wn[sub] = (w * (1.0 / 3.0)).astype(jnp.bfloat16)

            @pl.when(jnp.logical_not(summed))
            def _():
                w = fresh(wn[sub], f0) + own + fresh(wo[sub], f2)
                wn[sub] = (w * (1.0 / 3.0)).astype(jnp.bfloat16)

            fn[sub] = ((f0 + f1 + f2) * (1.0 / 3.0)).astype(jnp.bfloat16)
            return 0

        lax.fori_loop(0, SEND // PIECE, piece, 0)
        return 0

    lax.fori_loop(0, LATE, mix, 0)
    rs_x.wait_recv()
    igv[...] = ((over_y(xl) + xrecv[...].astype(jnp.float32)) * scale).astype(jnp.bfloat16)
    lax.fori_loop(LATE, sends, mix, 0)

    def drain(n, _):
        blk = rows_of(n)
        send_near(blk, n).wait_send()
        send_out(blk, n).wait_send()
        return 0

    lax.fori_loop(0, sends, drain, 0)
    def sent(mine, theirs):
        for cp in near_rows(theirs) + out_rows(mine) + [sums(mine)]:
            cp.wait_send()

    by_kind(sent)
    gathers = [ag_x, *ag_y0, *ag_y0p, *ag_y1, *ag_y1p, ag_c0, ag_c1]
    for cp in gathers + [rs_c, *transit, *ready, *joined, rs_x, w_near]:
        cp.wait_send()


def store(ig, mw, mm, ig_hbm, mw_hbm, mm_hbm, sem):
    copies = [pltpu.make_async_copy(ig, ig_hbm, sem.at[0])]
    part = mw.shape[0] // STORES
    for i in range(STORES):
        blk = pl.ds(i * part, part)
        copies.append(pltpu.make_async_copy(mw.at[blk], mw_hbm.at[blk], sem.at[1 + 2 * i]))
        copies.append(pltpu.make_async_copy(mm.at[blk], mm_hbm.at[blk], sem.at[2 + 2 * i]))
    for cp in copies:
        cp.start()
    for cp in copies:
        cp.wait()


def per_device(inputs, gate_pre, grad_hidden, up_weight, momentum):
    rows, depth = inputs.shape
    tokens, width = gate_pre.shape
    sends = depth // SEND
    bf = jnp.bfloat16
    any_spec = pl.BlockSpec(memory_space=pl.ANY)
    dma = pltpu.SemaphoreType.DMA
    big = pltpu.VMEM((depth, width), bf)
    ig, mw, mm = pl.pallas_call(
        kernel,
        out_shape=(pltpu.VMEM((rows, depth), bf), big, big),
        in_specs=[any_spec] * 5,
        out_specs=(pl.BlockSpec(memory_space=pltpu.VMEM),) * 3,
        scratch_shapes=[
            big,
            big,
            pltpu.VMEM((tokens, width), bf),
            pltpu.VMEM((2, 4, 2, rows, depth), bf),
            pltpu.VMEM((2, 4, 2, rows, depth), bf),
            pltpu.VMEM((2, 4, rows, depth), bf),
            pltpu.VMEM((2, 2, rows, depth), bf),
            pltpu.VMEM((2, rows // 2, depth), bf),
            pltpu.VMEM((2, rows // 2, depth), bf),
            pltpu.VMEM((rows, depth), bf),
            pltpu.VMEM((rows, depth), bf),
            big,
            big,
            pltpu.VMEM((max(sum(INNER_ROWS), sum(OUTER_ROWS)), width), bf),
            dma((5,)),
            dma((2, 3)),
            dma((2, 3)),
            dma((11,)),
            dma((11,)),
            dma((8,)),
            dma((8,)),
            dma((2, sends)),
            dma((2, sends)),
            dma((3,)),
            dma((3,)),
            pltpu.SemaphoreType.REGULAR((2,)),
        ],
        compiler_params=pltpu.CompilerParams(
            collective_id=0, has_side_effects=True, vmem_limit_bytes=50 * 2**20
        ),
        name="step",
    )(inputs, gate_pre, grad_hidden, up_weight[0], momentum[0])
    whole = jax.ShapeDtypeStruct((depth, width), bf)
    ig, mw, mm = pl.pallas_call(
        store,
        out_shape=(jax.ShapeDtypeStruct((rows, depth), bf), whole, whole),
        in_specs=[any_spec] * 3,
        out_specs=(any_spec,) * 3,
        scratch_shapes=[dma((1 + 2 * STORES,))],
        compiler_params=pltpu.CompilerParams(vmem_limit_bytes=2**20),
        name="store",
    )(ig, mw, mm)
    return ig, mw[None], mm[None]


def solution(mesh):
    in_specs = (
        P(("rep", "tp"), None),
        P("rep", "tp"),
        P("rep", "tp"),
        P("rep", None, "tp"),
        P("rep", None, "tp"),
    )
    out_specs = (P(("rep", "tp"), None), P("rep", None, "tp"), P("rep", None, "tp"))
    return jax.shard_map(
        per_device, mesh=mesh, in_specs=in_specs, out_specs=out_specs, check_vma=False
    )
```
